512 devices in a mesh: bx: 8 (over x, core), by: 16 (over z), rhs: 4 (over y).
Axes of the slice: x: 4, y: 4, z: 16, core: 2. Of those that a mesh axis runs over, the one named last changes fastest.
Arguments:
- rhs_nodes: float32 [8, 16, 64, 256], P('bx', 'by', 'rhs'), may hold values from -6 to 6
- forward: float32 [8, 16, 64, 256], P('bx', 'by', 'rhs'), may hold values from -6 to 6
- leaf_map: float32 [8, 16, 256, 256], P('bx', 'by'), may hold values from -0.375 to 0.375
- derivative: float32 [8, 16, 256, 256], P('bx', 'by'), may hold values from -0.375 to 0.375
- node_panel: int32 [8, 16, 256], P('bx', 'by'), may hold values from 0 to 15, never falling along the last dimension, each value on 1 to 32 neighbouring positions
- order_one: int32 [8, 16, 256], P('bx', 'by'), may hold values from 0 to 255, each once within a row
- near_one: int32 [8, 16, 9], P('bx', 'by'), may hold values 0 or 1
- interp_one: float32 [8, 16, 128, 128], P('bx', 'by'), may hold values from -0.25 to 0.25
- solve_one: float32 [8, 16, 128, 128], P('bx', 'by')
- couple_one: float32 [8, 16, 9, 128, 128], P('bx', 'by'), may hold values from -0.09375 to 0.09375
- back_one: float32 [8, 16, 128, 128], P('bx', 'by'), may hold values from -0.25 to 0.25
- spread_one: float32 [8, 16, 9, 128, 128], P('bx', 'by'), may hold values from -0.09375 to 0.09375
- order_two: int32 [8, 16, 256], P('bx', 'by'), may hold values from 0 to 255, as said below
- interp_two: float32 [8, 16, 128, 64], P('bx', 'by'), may hold values from -0.25 to 0.25
- solve_two: float32 [8, 16, 128, 64], P('bx', 'by')
- couple_two: float32 [8, 16, 9, 128, 64], P('bx', 'by'), may hold values from -0.09375 to 0.09375
- back_two: float32 [8, 16, 128, 64], P('bx', 'by'), may hold values from -0.25 to 0.25
- spread_two: float32 [8, 16, 9, 128, 64], P('bx', 'by'), may hold values from -0.09375 to 0.09375
- order_three: int32 [8, 16, 256], P('bx', 'by'), may hold values from 0 to 255, as said below
- interp_three: float32 [8, 16, 128, 32], P('bx', 'by'), may hold values from -0.25 to 0.25
- solve_three: float32 [8, 16, 128, 32], P('bx', 'by')
- couple_three: float32 [8, 16, 9, 128, 32], P('bx', 'by'), may hold values from -0.09375 to 0.09375
- back_three: float32 [8, 16, 128, 32], P('bx', 'by'), may hold values from -0.25 to 0.25
- spread_three: float32 [8, 16, 9, 128, 32], P('bx', 'by'), may hold values from -0.09375 to 0.09375
- top_three: float32 [8, 16, 128, 32], P('bx', 'by')
Outputs:
- adjoint: float32 [8, 16, 64, 256], P('bx', 'by', 'rhs')
- gradient: float32 [8, 16, 16], P('bx', 'by', 'rhs')
The draws below stay inside these ranges and needn't reach their ends.
Inputs may be any that keep to these rules, and one draw needn't show every extreme that they name: `order_one`: each box's row is a permutation; the first 128 entries are its skeleton set, the rest its redundant set. `order_two`: each row is a permutation of the candidates of a second-level box; rows 2m and 2m + 1 of the same x are equal. `order_three`: each row is a permutation of the candidates of a third-level box; the four rows of one third-level box are equal. `node_panel`: never falling along a box's nodes; every panel has one or more nodes.
All inputs are finite; a program needn't handle non-finite values. No bound on the sum of `near_one` on one device may be relied on, other than what follows from the above.
Results may differ from the reference program's by a relative error of at most 0.00022.
Values sent between devices are 32-bit elements; how exact they have to be, the bound alone decides.
No kernel may reach another device: no remote copies, remote signals or barrier semaphores. Data moves between devices by JAX's collectives and lax.ppermute only.
A program may use at most 64 MiB of HBM per device.

```python
import math
import jax
import jax.numpy as jnp
import numpy as np
from jax import lax

K = 128
CAND = 256
NODE = 256
PANELS = 16
COLS = 64
GX = 8
GY = 16


def with_identity(noise, offset):
    rows_index = lax.broadcasted_iota(jnp.int32, noise.shape, noise.ndim - 2)
    cols_index = lax.broadcasted_iota(jnp.int32, noise.shape, noise.ndim - 1)
    return jnp.where(rows_index == cols_index + offset, 1.0, 0.0).astype(jnp.float32) + noise


def half_offset(shape):
    return lax.broadcasted_iota(jnp.int32, shape, 1) % 2 * (K // 2)


def quarter_offset(shape):
    first = lax.broadcasted_iota(jnp.int32, shape, 0) % 2
    second = lax.broadcasted_iota(jnp.int32, shape, 1) % 2
    return (2 * first + second) * (K // 4)


def box_orders(key, count):
    keys = jax.random.split(key, count)

    def single(subkey):
        return jax.random.permutation(subkey, 2 * K)
    return jax.vmap(single)(keys).astype(jnp.int32)


def draw_solve_one(key, part):
    key = jax.random.fold_in(key, 1)
    shape = (GX, GY, K, K)
    noise = 0.5 * jax.random.normal(key, shape, jnp.float32) / math.sqrt(K)
    return with_identity(noise, 0)


def draw_solve_two(key, part):
    key = jax.random.fold_in(key, 2)
    shape = (GX, GY, K, K // 2)
    noise = 0.5 * jax.random.normal(key, shape, jnp.float32) / math.sqrt(K)
    return with_identity(noise, half_offset((GX, GY, 1, 1)))


def draw_solve_three(key, part):
    key = jax.random.fold_in(key, 3)
    shape = (GX, GY, K, K // 4)
    noise = 0.5 * jax.random.normal(key, shape, jnp.float32) / math.sqrt(K)
    return with_identity(noise, quarter_offset((GX, GY, 1, 1)))


def draw_top_three(key, part):
    key = jax.random.fold_in(key, 4)
    shape = (GX, GY, K, K // 4)
    noise = 0.5 * jax.random.normal(key, shape, jnp.float32) / math.sqrt(K)
    return with_identity(noise, quarter_offset((GX, GY, 1, 1)))


def draw_order_two(key, part):
    key = jax.random.fold_in(key, 5)
    orders = box_orders(key, GX * (GY // 2)).reshape(GX, GY // 2, 2 * K)
    return jnp.repeat(orders, 2, axis=1)


def draw_order_three(key, part):
    key = jax.random.fold_in(key, 6)
    orders = box_orders(key, GX // 2 * (GY // 2)).reshape(GX // 2, GY // 2, 2 * K)
    return jnp.repeat(jnp.repeat(orders, 2, axis=0), 2, axis=1)


def plant(result, rng, low, largest):
    longest = result.shape.index(max(result.shape))
    spots = []
    for shift in (0, 1):
        where = [jax.random.randint(jax.random.fold_in(rng, axis), (), 0, length) for axis, length in enumerate(result.shape)]
        where[longest] = (where[longest] + shift) % result.shape[longest]
        spots.append(tuple(where))
    return result.at[spots[0]].set(low).at[spots[1]].set(largest)


def shard_levels(stream_key, extent, shards, smallest, high):
    def one(dim, blocks):
        draws = jax.random.uniform(jax.random.fold_in(jax.random.fold_in(stream_key, 6), dim), (blocks,), jnp.float32, smallest / len(shards), high / len(shards))
        return jnp.repeat(jnp.exp(draws), extent[dim] // blocks).reshape((-1,) + (1,) * (len(extent) - dim - 1))

    gain = one(*shards[0])
    for cut in shards[1:]:
        gain = gain * one(*cut)
    return gain


def length_profile(count, total, bound, skew):
    weights = [(1 << 20) // math.isqrt(grade ** skew) + 1 for grade in range(2, count + 1)]
    rest, given = total - bound - (count - 1), [1] * (count - 1)
    while rest > 0:
        movable = [i for i in range(count - 1) if given[i] < bound]
        pool, left = sum([weights[i] for i in movable]), rest
        for i in movable:
            extra = min(bound - given[i], max(1, left * weights[i] // pool), rest)
            given[i] = given[i] + extra
            rest = rest - extra
    return np.array([bound] + given)


def ragged_sizes(rng, amount, total, reach, slope):
    if amount == 2:
        one = jax.random.randint(rng, (), max(1, total - reach), min(reach, total - 1) + 1)
        return jnp.stack([one, total - one])
    tallies = jnp.asarray(length_profile(amount, total, reach, slope), jnp.int32)
    couples = (amount - 1) // 2
    source_of, sink = tallies[1:1 + 2 * couples:2], tallies[2:2 + 2 * couples:2]
    room = jnp.minimum(source_of - 1, reach - sink)
    passed = jax.random.randint(jax.random.fold_in(rng, 1), (couples,), 0, 1 << 20) % (room + 1)
    tallies = tallies.at[1:1 + 2 * couples:2].set(source_of - passed).at[2:2 + 2 * couples:2].set(sink + passed)
    return tallies[jax.random.permutation(jax.random.fold_in(rng, 2), amount)]


def normal_values(own_key, dims, spread, most, cuts=(), kind=jnp.bfloat16):
    values = spread * jax.random.normal(own_key, dims, jnp.float32)
    if cuts:
        values = values * shard_levels(own_key, dims, cuts, -0.22, 0.18)
    return jnp.clip(values, -most, most).astype(kind)


def setup_inputs(seed: int = 0) -> dict:
    arg_keys = jax.random.split(jax.random.key(seed), 26)
    return {
        "rhs_nodes": normal_values(arg_keys[0], (GX, GY, COLS, NODE), 1.0, 6.0, ((0, 8), (1, 16), (2, 4)), jnp.float32),
        "forward": normal_values(arg_keys[1], (GX, GY, COLS, NODE), 1.0, 6.0, ((0, 8), (1, 16), (2, 4)), jnp.float32),
        "leaf_map": normal_values(arg_keys[2], (GX, GY, CAND, NODE), NODE ** -0.5, 0.375, ((0, 8), (1, 16)), jnp.float32),
        "derivative": normal_values(arg_keys[3], (GX, GY, NODE, NODE), NODE ** -0.5, 0.375, ((0, 8), (1, 16)), jnp.float32),
        "node_panel": jax.vmap(lambda own: jnp.searchsorted(jnp.cumsum(ragged_sizes(own, PANELS, NODE, 2 * NODE // PANELS, 1)), jnp.arange(NODE), side="right"))(jax.random.split(arg_keys[4], GX * GY)).reshape((GX, GY, NODE)).astype(jnp.int32),
        "order_one": jax.vmap(lambda own: jax.random.permutation(own, CAND))(jax.random.split(arg_keys[5], GX * GY)).reshape((GX, GY, CAND)).astype(jnp.int32),
        "near_one": plant((jax.random.randint(arg_keys[6], (GX, GY, 9), 0, 4) < 3).astype(jnp.int32), jax.random.fold_in(arg_keys[6], 1), 0, 1),
        "interp_one": normal_values(arg_keys[7], (GX, GY, K, K), (4 * K) ** -0.5, 0.25, ((0, 8), (1, 16)), jnp.float32),
        "solve_one": draw_solve_one(jax.random.fold_in(arg_keys[25], 71), 0),
        "couple_one": normal_values(arg_keys[9], (GX, GY, 9, K, K), (36 * K) ** -0.5, 0.09375, ((0, 8), (1, 16)), jnp.float32),
        "back_one": normal_values(arg_keys[10], (GX, GY, K, K), (4 * K) ** -0.5, 0.25, ((0, 8), (1, 16)), jnp.float32),
        "spread_one": normal_values(arg_keys[11], (GX, GY, 9, K, K), (36 * K) ** -0.5, 0.09375, ((0, 8), (1, 16)), jnp.float32),
        "order_two": draw_order_two(jax.random.fold_in(arg_keys[25], 71), 0),
        "interp_two": normal_values(arg_keys[13], (GX, GY, K, K // 2), (4 * K) ** -0.5, 0.25, ((0, 8), (1, 16)), jnp.float32),
        "solve_two": draw_solve_two(jax.random.fold_in(arg_keys[25], 71), 0),
        "couple_two": normal_values(arg_keys[15], (GX, GY, 9, K, K // 2), (36 * K) ** -0.5, 0.09375, ((0, 8), (1, 16)), jnp.float32),
        "back_two": normal_values(arg_keys[16], (GX, GY, K, K // 2), (4 * K) ** -0.5, 0.25, ((0, 8), (1, 16)), jnp.float32),
        "spread_two": normal_values(arg_keys[17], (GX, GY, 9, K, K // 2), (36 * K) ** -0.5, 0.09375, ((0, 8), (1, 16)), jnp.float32),
        "order_three": draw_order_three(jax.random.fold_in(arg_keys[25], 71), 0),
        "interp_three": normal_values(arg_keys[19], (GX, GY, K, K // 4), (4 * K) ** -0.5, 0.25, ((0, 8), (1, 16)), jnp.float32),
        "solve_three": draw_solve_three(jax.random.fold_in(arg_keys[25], 71), 0),
        "couple_three": normal_values(arg_keys[21], (GX, GY, 9, K, K // 4), (36 * K) ** -0.5, 0.09375, ((0, 8), (1, 16)), jnp.float32),
        "back_three": normal_values(arg_keys[22], (GX, GY, K, K // 4), (4 * K) ** -0.5, 0.25, ((0, 8), (1, 16)), jnp.float32),
        "spread_three": normal_values(arg_keys[23], (GX, GY, 9, K, K // 4), (36 * K) ** -0.5, 0.09375, ((0, 8), (1, 16)), jnp.float32),
        "top_three": draw_top_three(jax.random.fold_in(arg_keys[25], 71), 0),
    }


highest = lax.Precision.HIGHEST


def beside_all(values):
    padded = jnp.pad(values, ((1, 1), (1, 1)) + ((0, 0),) * (values.ndim - 2))
    grid_rows = values.shape[0]
    grid_cols = values.shape[1]
    blocks = [padded[1 + step_x:1 + step_x + grid_rows, 1 + step_y:1 + step_y + grid_cols] for step_x in (-1, 0, 1) for step_y in (-1, 0, 1)]
    return jnp.stack(blocks, axis=2)


def picked_cols(values, order):
    index = jnp.broadcast_to(order[:, :, None, :], values.shape[:3] + order.shape[-1:])
    return jnp.take_along_axis(values, index, axis=3)


def placed_cols(values, order):
    return picked_cols(values, jnp.argsort(order, axis=-1).astype(jnp.int32))


def product(values, blocks):
    return jnp.einsum("xycr,xyrk->xyck", values, blocks, precision=highest)


def nearby(stacked, blocks):
    return jnp.einsum("xyncr,xynrk->xyck", stacked, blocks, precision=highest)


def join_rows(values):
    shape = values.shape
    grouped = values.reshape((shape[0], shape[1] // 2, 2) + shape[2:])
    grouped = jnp.moveaxis(grouped, 2, -2)
    return grouped.reshape(grouped.shape[:-2] + (2 * shape[-1],))


def join_cols(values):
    shape = values.shape
    grouped = values.reshape((shape[0] // 2, 2) + shape[1:])
    grouped = jnp.moveaxis(grouped, 1, -2)
    return grouped.reshape(grouped.shape[:-2] + (2 * shape[-1],))


def whole_box(values):
    return join_cols(join_rows(values))


def split_cols(values):
    shape = values.shape
    grouped = values.reshape(shape[:-1] + (2, shape[-1] // 2))
    grouped = jnp.moveaxis(grouped, 3, 1)
    return grouped.reshape((shape[0] * 2, shape[1], shape[2], shape[-1] // 2))


def split_rows(values):
    shape = values.shape
    grouped = values.reshape(shape[:-1] + (2, shape[-1] // 2))
    grouped = jnp.moveaxis(grouped, 3, 2)
    return grouped.reshape((shape[0], shape[1] * 2, shape[2], shape[-1] // 2))


def reference(rhs_nodes, forward, leaf_map, derivative, node_panel, order_one, near_one, interp_one, solve_one, couple_one, back_one, spread_one, order_two, interp_two, solve_two, couple_two, back_two, spread_two, order_three, interp_three, solve_three, couple_three, back_three, spread_three, top_three):
    weights = near_one.astype(jnp.float32)[:, :, :, None, None]
    cand = jnp.einsum("xycn,xykn->xyck", rhs_nodes, leaf_map, precision=highest)
    picked = picked_cols(cand, order_one)
    redund = picked[..., K:]
    zone_one = product(redund, solve_one)
    skel_one = picked[..., :K] - product(redund, interp_one) - nearby(weights * beside_all(zone_one), couple_one)
    order_box = order_two[:, ::2]
    picked = picked_cols(join_rows(skel_one), order_box)
    redund = picked[..., K:]
    zone_two = product(redund, join_rows(solve_two))
    skel_two = picked[..., :K] - product(redund, join_rows(interp_two)) - nearby(beside_all(zone_two), join_rows(couple_two))
    order_top = order_three[::2, ::2]
    picked = picked_cols(join_cols(skel_two), order_top)
    redund = picked[..., K:]
    zone_three = product(redund, whole_box(solve_three))
    skel_three = picked[..., :K] - product(redund, whole_box(interp_three)) - nearby(beside_all(zone_three), whole_box(couple_three))
    value_three = product(skel_three, whole_box(top_three))
    rest_three = zone_three - product(value_three, whole_box(back_three)) - nearby(beside_all(value_three), whole_box(spread_three))
    final_three = placed_cols(jnp.concatenate([value_three, rest_three], -1), order_top)
    value_two = split_cols(final_three)
    rest_two = zone_two - product(value_two, join_rows(back_two)) - nearby(beside_all(value_two), join_rows(spread_two))
    final_two = placed_cols(jnp.concatenate([value_two, rest_two], -1), order_box)
    value_one = split_rows(final_two)
    rest_one = zone_one - product(value_one, back_one) - nearby(weights * beside_all(value_one), spread_one)
    final_one = placed_cols(jnp.concatenate([value_one, rest_one], -1), order_one)
    adjoint = jnp.einsum("xyck,xykn->xycn", final_one, leaf_map, precision=highest)
    field = jnp.einsum("xycm,xymn->xycn", forward, derivative, precision=highest)
    summed = jnp.sum(adjoint * field, axis=2) / adjoint.shape[2]
    member = (node_panel[..., None] == jnp.arange(PANELS, dtype=jnp.int32)).astype(jnp.float32)
    gradient = jnp.einsum("xyn,xynp->xyp", summed, member, precision=highest)
    return adjoint, gradient
```

```python
import functools

import jax
import jax.numpy as jnp
from jax import lax
from jax.sharding import PartitionSpec as P

PANELS = 16
AXES = ("bx", "by", "rhs")
PRECISION = lax.Precision.HIGH


def dot(left, right):
    return lax.dot_general(
        left, right, (((1,), (0,)), ((), ())), precision=PRECISION, preferred_element_type=jnp.float32
    )


def dot_t(left, right):
    return lax.dot_general(
        left, right, (((1,), (1,)), ((), ())), precision=PRECISION, preferred_element_type=jnp.float32
    )


def lanes(*parts):
    return jnp.concatenate(parts, axis=-1)


def rows(*parts):
    return jnp.concatenate(parts, axis=0)


class Groups:
    def __init__(self, size_x, size_y, size_r):
        def place(i, j, r):
            return (i * size_y + j) * size_r + r

        every = [(i, j, r) for i in range(size_x) for j in range(size_y) for r in range(size_r)]
        self.sibling = [[place(i, j, r), place(i + 1, j, r)] for i, j, r in every if i % 2 == 0]
        self.diagonal = [[place(i, j, r), place(i + 1, j ^ 1, r)] for i, j, r in every if i % 2 == 0]
        self.shifted = []
        for j in range(1, size_y, 2):
            after = (j + 1) % size_y
            for r in range(size_r):
                for i in range(1, size_x - 1, 2):
                    self.shifted.append(
                        [place(i, j, r), place(i, after, r), place(i + 1, j, r), place(i + 1, after, r)]
                    )
                if r % 2 == 0:
                    for i in (0, size_x - 1):
                        self.shifted.append(
                            [place(i, j, r), place(i, after, r), place(i, j, r + 1), place(i, after, r + 1)]
                        )


def on_device(
    groups,
    rhs_nodes,
    forward,
    leaf_map,
    derivative,
    node_panel,
    order_one,
    near_one,
    interp_one,
    solve_one,
    couple_one,
    back_one,
    spread_one,
    order_two,
    interp_two,
    solve_two,
    couple_two,
    back_two,
    spread_two,
    order_three,
    interp_three,
    solve_three,
    couple_three,
    back_three,
    spread_three,
    top_three,
):
    skel = interp_one.shape[-1]
    half, quarter = skel // 2, skel // 4
    size_x, size_y = lax.axis_size("bx"), lax.axis_size("by")
    place_x, place_y, place_r = (lax.axis_index(axis) for axis in AXES)
    upper_x, upper_y = place_x % 2 == 1, place_y % 2 == 1
    same = upper_x == upper_y
    edge_x = (place_x == 0) | (place_x == size_x - 1)
    edge_y = (place_y == 0) | (place_y == size_y - 1)
    slot_x = jnp.where(edge_x, place_r % 2 == 1, ~upper_x)
    slot_y = ~upper_y
    lane = lax.broadcasted_iota(jnp.int32, (1, skel), 1)
    own_half = (lane // half) == place_y % 2
    own_quarter = (lane // quarter) == 2 * (place_x % 2) + place_y % 2

    def relative(blocks):
        cube = blocks.reshape((3, 3) + blocks.shape[1:])
        cube = jnp.where(upper_x, cube, cube[::-1])
        return jnp.where(upper_y, cube, cube[:, ::-1])

    def member(order):
        return (order[:, None] == lax.broadcasted_iota(jnp.int32, (1, order.shape[0]), 1)).astype(jnp.float32)

    def pick(values, chosen):
        return dot_t(values, chosen)

    def both(values, axis_groups):
        return lax.all_gather(values, AXES, axis_index_groups=axis_groups)

    def other_of(pair):
        return jnp.where(upper_x, pair[0], pair[1])

    def outside(along, across):
        toward = jnp.stack([along, across])
        first = jnp.where(slot_y, toward[1], toward[0])
        second = jnp.where(slot_y, toward[0], toward[1])
        got = lax.all_to_all(
            jnp.stack([first, second, first, second]), AXES, 0, 0, axis_index_groups=groups.shifted
        )
        beside = jnp.where(slot_x, got[:2], got[2:])
        mine = jnp.where(slot_x, got[2:], got[:2])
        out_x = jnp.where(slot_y, beside[1], beside[0])
        out_xy = jnp.where(slot_y, beside[0], beside[1])
        out_y = jnp.where(slot_y, mine[0], mine[1])
        return (
            jnp.where(edge_x, 0.0, out_x),
            jnp.where(edge_y, 0.0, out_y),
            jnp.where(edge_x | edge_y, 0.0, out_xy),
        )

    near = near_one[0, 0].astype(jnp.float32)[:, None, None]
    blocks_one = relative(near * couple_one[0, 0])
    blocks_two = relative(couple_two[0, 0])
    blocks_three = relative(couple_three[0, 0])
    lift_one = relative(near * spread_one[0, 0])
    lift_two = relative(spread_two[0, 0])
    lift_three = relative(spread_three[0, 0])

    def third(corner, edge):
        return lanes(blocks_three[corner], blocks_three[edge], lift_three[corner], lift_three[edge])

    inverses = lanes(solve_two[0, 0], solve_three[0, 0], top_three[0, 0])
    to_row = [
        blocks_one[1, 0],
        blocks_one[2, 0],
        blocks_one[0, 0],
        inverses,
        jnp.where(same, third((2, 0), (1, 0)), third((2, 0), (2, 1))),
        jnp.where(same, third((0, 0), (0, 1)), third((0, 0), (1, 0))),
    ] + [lanes(blocks_two[side, 0], lift_two[side, 0]) for side in range(3)]
    swap = [(i, i ^ 1) for i in range(size_y)]
    row = lax.ppermute(jnp.stack(to_row), "by", swap)

    chosen_one = member(order_one[0, 0])
    candidates = dot_t(rhs_nodes[0, 0], leaf_map[0, 0])
    picked_one = pick(candidates, chosen_one)
    redund_one = picked_one[:, skel:]
    zone_one = dot(redund_one, solve_one[0, 0])
    base_one = picked_one[:, :skel] - dot(redund_one, interp_one[0, 0])
    field = dot(forward[0, 0], derivative[0, 0])

    out_x, out_y, out_xy = outside(zone_one, zone_one)

    to_side = jnp.stack(
        [
            blocks_one[0, 1],
            blocks_one[0, 2],
            row[2],
            inverses,
            row[3],
            jnp.where(same, third((0, 2), (1, 2)), third((0, 2), (0, 1))),
            row[5],
        ]
    )
    orders = order_two[0, 0].astype(jnp.float32).reshape(1, 2, skel)
    orders = jnp.pad(orders, ((0, 0), (0, skel - 2), (0, 0)))
    side = other_of(both(rows(to_side, orders), groups.sibling))

    part_own = base_one - dot(
        lanes(zone_one, out_x, out_y, out_xy),
        rows(blocks_one[1, 1], blocks_one[2, 1], blocks_one[1, 2], blocks_one[2, 2]),
    )
    part_side = -dot(lanes(zone_one, out_y), rows(side[0], side[1]))
    part_row = -dot(lanes(zone_one, out_x), rows(row[0], row[1]))
    part_diag = -dot(zone_one, side[2])
    parts = jnp.stack([part_own, part_side, part_row, part_diag])
    parts = parts + other_of(both(parts, groups.diagonal))[::-1]
    parts = parts + other_of(both(parts, groups.sibling))[jnp.array([1, 0, 3, 2])]

    def by_row(first, second):
        return jnp.where(upper_y, lanes(second, first), lanes(first, second))

    def by_side(first, second):
        return jnp.where(upper_x, lanes(second, first), lanes(first, second))

    chosen_two = member(order_two[0, 0])
    chosen_side = member(side[7, :2].reshape(-1).astype(jnp.int32))
    solve_own = by_row(solve_two[0, 0], row[3][:, :half])
    solve_side = by_row(side[3][:, :half], side[4][:, :half])
    picked_two = pick(by_row(parts[0], parts[2]), chosen_two)
    redund_two = picked_two[:, skel:]
    zone_two = dot(redund_two, solve_own)
    redund_side = pick(by_row(parts[1], parts[3]), chosen_side[skel:])
    zone_side = dot(redund_side, solve_side)

    def second_level(values_own, values_side, kept, native, far):
        gone_x, gone_y, gone_xy = outside(
            jnp.stack([values_own, values_side]), jnp.stack([values_own, values_side])
        )
        here = dot(lanes(*kept[0], values_side, values_own, gone_x[0]), rows(*kept[1], *native))
        beyond = dot(lanes(gone_y[1], gone_y[0], gone_xy[0]), rows(*far))
        return here, beyond

    def all_parts(part):
        pair = jnp.stack([part, other_of(both(part, groups.diagonal))])
        return pair + other_of(both(pair, groups.sibling))[::-1]

    here, beyond = second_level(
        zone_two,
        zone_side,
        ([redund_two], [interp_two[0, 0]]),
        [blocks_two[a, 1] for a in range(3)],
        [by_row(blocks_two[a, 2], row[6 + a][:, :half]) for a in range(3)],
    )
    part = jnp.where(own_half, picked_two[:, :skel] - lanes(here, here), 0.0) - beyond
    skel_two = all_parts(part)

    def by_box(own, along, across, far):
        return jnp.where(
            upper_x,
            by_row_pairs(along, far, own, across),
            by_row_pairs(own, across, along, far),
        )

    def by_row_pairs(first, second, third_, fourth):
        return lanes(by_row(first, second), by_row(third_, fourth))

    def quarters(place):
        return [where[:, place * quarter : (place + 1) * quarter] for where in (side[5], row[4], side[6])]

    def whole(own, place):
        along, across, far = quarters(place)
        return by_box(own, along, across, far)

    corner_down, corner_up = whole(blocks_three[2, 2], 0), whole(lift_three[2, 2], 2)
    edge_down = whole(jnp.where(same, blocks_three[2, 1], blocks_three[1, 2]), 1)
    edge_up = whole(jnp.where(same, lift_three[2, 1], lift_three[1, 2]), 3)
    solve_whole = by_box(
        *[part_[:, half : half + quarter] for part_ in (inverses, side[3], row[3], side[4])]
    )
    top_whole = by_box(*[part_[:, half + quarter :] for part_ in (inverses, side[3], row[3], side[4])])

    chosen_three = member(order_three[0, 0])
    picked_three = pick(by_side(skel_two[0], skel_two[1]), chosen_three)
    redund_three = picked_three[:, skel:]
    zone_three = dot(redund_three, solve_whole)

    def third_level(values, corner, edge):
        gone_x, gone_y, gone_xy = outside(values, values)
        return dot(lanes(gone_xy, jnp.where(same, gone_x, gone_y)), rows(corner, edge))

    def total(part):
        part = part + other_of(both(part, groups.diagonal))
        return part + other_of(both(part, groups.sibling))

    def tiled(values):
        return lanes(values, values, values, values)

    here = dot(lanes(redund_three, zone_three), rows(interp_three[0, 0], blocks_three[1, 1]))
    part = jnp.where(own_quarter, picked_three[:, :skel] - tiled(here), 0.0)
    skel_three = total(part - third_level(zone_three, corner_down, edge_down))
    value_three = dot(skel_three, top_whole)

    here = dot(value_three, back_three[0, 0] + lift_three[1, 1])
    part = jnp.where(own_quarter, zone_three - tiled(here), 0.0)
    rest_three = total(part - third_level(value_three, corner_up, edge_up))
    final_three = dot(lanes(value_three, rest_three), chosen_three)

    low, high = final_three[:, :skel], final_three[:, skel:]
    value_two = jnp.where(upper_x, high, low)
    value_side = jnp.where(upper_x, low, high)
    here, beyond = second_level(
        value_two,
        value_side,
        ([], []),
        [lift_two[0, 1], lift_two[1, 1] + back_two[0, 0], lift_two[2, 1]],
        [by_row(lift_two[a, 2], row[6 + a][:, half:]) for a in range(3)],
    )
    part = jnp.where(own_half, zone_two - lanes(here, here), 0.0) - beyond
    rest_two = all_parts(part)
    final_two = dot(lanes(value_two, rest_two[0]), chosen_two)
    final_side = dot(lanes(value_side, rest_two[1]), chosen_side)

    def rows_of(final):
        low, high = final[:, :skel], final[:, skel:]
        return jnp.where(upper_y, high, low), jnp.where(upper_y, low, high)

    value_own, value_row = rows_of(final_two)
    value_along, value_diag = rows_of(final_side)
    gone_x, gone_y, gone_xy = outside(
        jnp.stack([value_own, value_row]), jnp.stack([value_own, value_along])
    )
    around = lanes(
        value_diag, value_along, gone_y[1], value_row, value_own, gone_y[0], gone_x[1], gone_x[0], gone_xy[0]
    )
    lifts = [lift_one[a, b] for a in range(3) for b in range(3)]
    lifts[4] = lifts[4] + back_one[0, 0]
    rest_one = zone_one - dot(around, rows(*lifts))
    final_one = dot(lanes(value_own, rest_one), chosen_one)
    adjoint = dot(final_one, leaf_map[0, 0])

    count = lax.axis_size("rhs")
    weight = jnp.sum(adjoint * field, axis=0, keepdims=True) / (count * adjoint.shape[0])
    panel = lax.broadcasted_iota(jnp.int32, (PANELS, 1), 0)
    inside = (node_panel[0] == panel).astype(jnp.float32)
    shares = dot_t(weight, inside).reshape(count, PANELS // count)
    shares = lax.all_to_all(shares, "rhs", 0, 0, tiled=True)
    gradient = jnp.sum(shares, axis=0)
    return adjoint[None, None], gradient[None, None]


def solution(mesh):
    box = P("bx", "by")
    columns = P("bx", "by", "rhs", None)
    groups = Groups(mesh.shape["bx"], mesh.shape["by"], mesh.shape["rhs"])
    return jax.shard_map(
        functools.partial(on_device, groups),
        mesh=mesh,
        in_specs=(columns, columns) + (box,) * 23,
        out_specs=(columns, P("bx", "by", "rhs")),
        check_vma=False,
    )
```

```python
import functools

import jax
import jax.numpy as jnp
from jax import lax
from jax.experimental import pallas as pl
from jax.experimental.pallas import tpu as pltpu
from jax.sharding import PartitionSpec as P

PANELS = 16
SKEL = 128
HALF = SKEL // 2
QUARTER = SKEL // 4
BOX = 2 * SKEL
COLS = 16
VMEM_LIMIT = 8 << 20
AXES = ("bx", "by", "rhs")
VALUES = (COLS, SKEL)
BLOCK = (SKEL, SKEL)


def halves(values):
    high = values.astype(jnp.bfloat16)
    low = (values - high.astype(jnp.float32)).astype(jnp.bfloat16)
    return high, low


def dims(left, rights, contract):
    left = jnp.concatenate(halves(left), axis=0)
    size = left.shape[0] // 2
    result = None
    for right in rights:
        product = lax.dot_general(
            left, right, (((1,), (contract,)), ((), ())), preferred_element_type=jnp.float32
        )
        product = product[:size] + product[size:]
        result = product if result is None else result + product
    return result


def dot(left, right):
    return dims(left, halves(right), 0)


def dot_t(left, right):
    return dims(left, halves(right), 1)


def pick(values, order):
    return dims(values, (chosen(order),), 0)


def place(values, order):
    return dims(values, (chosen(order),), 1)


def lanes(*parts):
    return jnp.concatenate(parts, axis=1)


def stacked(*parts):
    return jnp.concatenate(parts, axis=0)


class Groups:
    def __init__(self, size_x, size_y, size_r):
        def place(i, j, r):
            return (i * size_y + j) * size_r + r

        every = [(i, j, r) for i in range(size_x) for j in range(size_y) for r in range(size_r)]
        self.sibling = [[place(i, j, r), place(i + 1, j, r)] for i, j, r in every if i % 2 == 0]
        self.diagonal = [[place(i, j, r), place(i + 1, j ^ 1, r)] for i, j, r in every if i % 2 == 0]
        self.shifted = []
        self.crossed = []
        for j in range(1, size_y, 2):
            after = (j + 1) % size_y
            for r in range(size_r):
                for i in range(1, size_x - 1, 2):
                    self.shifted.append(
                        [place(i, j, r), place(i, after, r), place(i + 1, j, r), place(i + 1, after, r)]
                    )
                    self.crossed.append(
                        [place(i, j, r), place(i - 1, after, r), place(i + 1, j, r), place(i + 2, after, r)]
                    )
                if r % 2 == 0:
                    for i in (0, size_x - 1):
                        self.shifted.append(
                            [place(i, j, r), place(i, after, r), place(i, j, r + 1), place(i, after, r + 1)]
                        )
                        self.crossed.append(
                            [
                                place(i, j, r),
                                place(i ^ 1, after, r),
                                place(i, j, r + 1),
                                place(i ^ 1, after, r + 1),
                            ]
                        )


class Here:
    def __init__(self, crossed=False):
        x, y, r = (lax.axis_index(axis) for axis in AXES)
        self.c, self.h = lax.rem(x, 2), lax.rem(y, 2)
        side = jnp.where(self.h == 0, 1 - self.c, self.c) if crossed else self.c
        chip = x - self.c
        self.edge_x = ((chip == 0) & (side == 0)) | ((chip == lax.axis_size("bx") - 2) & (side == 1))
        self.edge_y = (y == 0) | (y == lax.axis_size("by") - 1)
        slot_x = jnp.where(self.edge_x, lax.rem(r, 2), 1 - side)
        slot_y = 1 - self.h
        self.slot_y = slot_y
        self.along = 2 * (1 - slot_x) + slot_y
        self.across = 2 * slot_x + 1 - slot_y
        self.corner = 2 * (1 - slot_x) + 1 - slot_y
        side_x = (2 - 2 * side, 1, 2 * side)
        side_y = (2 - 2 * self.h, 1, 2 * self.h)
        self.block = [[3 * a + b for b in side_y] for a in side_x]
        self.same = side == self.h

    def outside(self, got, item=()):
        x = jnp.where(self.edge_x, 0.0, got[(self.along, *item)])
        y = jnp.where(self.edge_y, 0.0, got[(self.across, *item)])
        xy = jnp.where(self.edge_x | self.edge_y, 0.0, got[(self.corner, *item)])
        return x, y, xy

    def by_row(self, own, other):
        return lanes(jnp.where(self.h == 0, own, other), jnp.where(self.h == 0, other, own))

    def own_half(self):
        lane = lax.broadcasted_iota(jnp.int32, VALUES, 1)
        return lane // HALF == self.h

    def own_quarter(self):
        lane = lax.broadcasted_iota(jnp.int32, VALUES, 1)
        return lane // QUARTER == 2 * self.c + self.h


def chosen(order):
    found = lax.broadcasted_iota(jnp.int32, (BOX, BOX), 0) == order
    return jnp.where(found, 1.0, 0.0).astype(jnp.bfloat16)


def four(values):
    return stacked(values, values, values, values)


NAMES = (
    "rhs_nodes",
    "leaf_map",
    "order_one",
    "solve_one",
    "interp_one",
    "near_one",
    "couple_one",
    "spread_one",
    "couple_two",
    "spread_two",
    "couple_three",
    "spread_three",
    "solve_two",
    "solve_three",
    "top_three",
    "interp_two",
    "interp_three",
    "back_one",
    "back_two",
    "back_three",
    "order_two",
    "order_three",
    "node_panel",
    "forward",
    "derivative",
)
GIVEN = (
    "rhs_nodes",
    "forward",
    "leaf_map",
    "derivative",
    "node_panel",
    "order_one",
    "near_one",
    "interp_one",
    "solve_one",
    "couple_one",
    "back_one",
    "spread_one",
    "order_two",
    "interp_two",
    "solve_two",
    "couple_two",
    "back_two",
    "spread_two",
    "order_three",
    "interp_three",
    "solve_three",
    "couple_three",
    "back_three",
    "spread_three",
    "top_three",
)

LIFT_ONE = 0
LEAF = LIFT_ONE + 9 * SKEL
COUPLE_TWO = LEAF + 2 * BOX
SPREAD_TWO = COUPLE_TWO + 6 * HALF
INTERP_TWO = SPREAD_TWO + 6 * HALF
SOLVE_TWO = INTERP_TWO + HALF
COUPLE_THREE = SOLVE_TWO + HALF
SPREAD_THREE = COUPLE_THREE + 3 * QUARTER
INTERP_THREE = SPREAD_THREE + 3 * QUARTER
SOLVE_THREE = INTERP_THREE + QUARTER
TOP_THREE = SOLVE_THREE + QUARTER
NUMBERS = TOP_THREE + QUARTER
FIELD = NUMBERS + 8
ZONE_ONE = FIELD + 2 * COLS
KEPT = (ZONE_ONE + COLS, SKEL)
ORDER_ONE, ORDER_TWO, ORDER_THREE, PANEL_OF = range(0, 8, 2)

SOLVE_OWN, SOLVE_SIDE, SOLVE_ALL, TOP_ALL, COUPLE_ALL, SPREAD_ALL = 0, 1, 2, 3, 4, 6
COUPLE_FAR, SPREAD_FAR, ORDER_SIDE = 8, 11, 14
WHOLE = (ORDER_SIDE * SKEL + 8, SKEL)
SIDE_BLOCKS = 2 * COLS
SIDE_NUMBERS = SIDE_BLOCKS + 3 * SKEL
SIDE = (SIDE_NUMBERS + 8, SKEL)


def numbers_of(ref, row):
    return lanes(ref[row : row + 1], ref[row + 1 : row + 2]).astype(jnp.int32)


def block_of(ref, number):
    return ref[number * SKEL : (number + 1) * SKEL]


def start_kernel(*refs):
    count = len(NAMES)
    source = dict(zip(NAMES, refs[:count]))
    zone, base, row_out, side_out, couple, kept = refs[count : count + 6]
    held = dict(zip(NAMES, refs[count + 6 : -1]))
    sems = refs[-1]
    here = Here()
    copies = {name: pltpu.make_async_copy(source[name], held[name], sems.at[i]) for i, name in enumerate(NAMES)}
    for name in NAMES:
        copies[name].start()

    def read(name):
        copies[name].wait()
        return held[name][...]

    rhs, leaf = read("rhs_nodes"), read("leaf_map")
    candidates = dot_t(rhs, leaf)
    kept[LEAF : LEAF + BOX] = leaf[:, :SKEL]
    kept[LEAF + BOX : LEAF + 2 * BOX] = leaf[:, SKEL:]
    picked = pick(candidates, read("order_one"))
    redund = picked[:, SKEL:]
    values = dot(redund, read("solve_one"))
    zone[...] = values
    kept[ZONE_ONE:] = values
    base[...] = picked[:, :SKEL] - dot(redund, read("interp_one"))
    spots = lax.broadcasted_iota(jnp.int32, (16, 9), 0) == lax.broadcasted_iota(jnp.int32, (16, 9), 1)
    near = jnp.where(spots, read("near_one").astype(jnp.float32), 0.0)
    near = jnp.broadcast_to(jnp.sum(near, axis=1, keepdims=True), VALUES)
    number = lax.broadcasted_iota(jnp.int32, VALUES, 0)

    def scaled(name, a, b):
        n = here.block[a][b]
        weight = jnp.sum(jnp.where(number == n, near, 0.0), axis=0, keepdims=True)
        return weight * held[name][n]

    for name in NAMES[NAMES.index("couple_one") :]:
        copies[name].wait()
    for out, start in ((row_out.at[0], 0), (side_out, 0)):
        out[start : start + HALF] = held["solve_two"][...]
        out[start + HALF : start + HALF + QUARTER] = held["solve_three"][...]
        out[start + HALF + QUARTER : start + SKEL] = held["top_three"][...]
    cross = Here(crossed=True)

    def third(out, start, corner, edge_same, edge_else):
        corner = cross.block[corner[0]][corner[1]]
        edge = jnp.where(
            cross.same, cross.block[edge_same[0]][edge_same[1]], cross.block[edge_else[0]][edge_else[1]]
        )
        for i, (name, n) in enumerate(
            (("couple_three", corner), ("couple_three", edge), ("spread_three", corner), ("spread_three", edge))
        ):
            out[start + i * QUARTER : start + (i + 1) * QUARTER] = held[name][n]

    third(row_out.at[1], 0, (0, 0), (0, 1), (1, 0))
    third(side_out, SKEL, (0, 2), (1, 2), (0, 1))
    third(side_out, 2 * SKEL, (2, 0), (1, 0), (2, 1))
    for a in range(3):
        n = here.block[a][0]
        row_out[2 + a, :HALF] = held["couple_two"][n]
        row_out[2 + a, HALF:] = held["spread_two"][n]
    for a in range(3):
        for b in range(3):
            at = (3 * a + b) * SKEL
            couple[at : at + SKEL] = scaled("couple_one", a, b)
            at = LIFT_ONE + at
            block = scaled("spread_one", a, b)
            kept[at : at + SKEL] = block + held["back_one"][...] if a == b == 1 else block
        for b in (1, 2):
            n = here.block[a][b]
            at = COUPLE_TWO + (2 * a + b - 1) * HALF
            kept[at : at + HALF] = held["couple_two"][n]
            at = SPREAD_TWO + (2 * a + b - 1) * HALF
            block = held["spread_two"][n]
            kept[at : at + HALF] = block + held["back_two"][...] if a == b == 1 else block
    edge = jnp.where(cross.same, cross.block[2][1], cross.block[1][2])
    for i, n in enumerate((4, cross.block[2][2], edge)):
        at = COUPLE_THREE + i * QUARTER
        kept[at : at + QUARTER] = held["couple_three"][n]
        at = SPREAD_THREE + i * QUARTER
        block = held["spread_three"][n]
        kept[at : at + QUARTER] = block + held["back_three"][...] if i == 0 else block
    for name, at in (
        ("interp_two", INTERP_TWO),
        ("solve_two", SOLVE_TWO),
        ("interp_three", INTERP_THREE),
        ("solve_three", SOLVE_THREE),
        ("top_three", TOP_THREE),
    ):
        kept[at : at + held[name].shape[0]] = held[name][...]
    for name, row in (
        ("order_one", ORDER_ONE),
        ("order_two", ORDER_TWO),
        ("order_three", ORDER_THREE),
        ("node_panel", PANEL_OF),
    ):
        numbers = held[name][...].astype(jnp.float32)
        kept[NUMBERS + row : NUMBERS + row + 1] = numbers[:, :SKEL]
        kept[NUMBERS + row + 1 : NUMBERS + row + 2] = numbers[:, SKEL:]
    side_out[3 * SKEL :] = kept[NUMBERS : NUMBERS + 8]
    field = dot(held["forward"][...], held["derivative"][...])
    kept[FIELD : FIELD + COLS] = field[:, :SKEL]
    kept[FIELD + COLS : FIELD + 2 * COLS] = field[:, SKEL:]


def side_kernel(pair, side, out):
    out[:COLS], out[COLS:SIDE_BLOCKS] = pair[0], pair[1]
    out[SIDE_BLOCKS:] = side[...]


def fill(here, boxes, chunk):
    for slot in range(4):
        chunk[slot, 0] = boxes[0]
        chunk[slot, 1] = jnp.where(here.slot_y == slot % 2, boxes[2], boxes[1])


def around(here, got, boxes):
    out_x, out_y, out_xy = here.outside(got, (0,))
    out_x_row = jnp.where(here.edge_x, 0.0, got[here.along, 1])
    out_y_side = jnp.where(here.edge_y, 0.0, got[here.across, 1])
    return lanes(boxes[3], boxes[1], out_y_side, boxes[2], boxes[0], out_y, out_x_row, out_x, out_xy)


def row_kernel(row, sides, chunk, boxes, out):
    here = Here()
    c, d = here.c, 1 - here.c
    for box, (member, number) in enumerate(((c, c), (d, d), (d, c), (c, d))):
        boxes[box] = sides[member, pl.ds(pl.multiple_of(number * COLS, COLS), COLS)]
    fill(here, boxes, chunk)
    out[0], out[1] = row[0], sides[d, SIDE_BLOCKS : SIDE_BLOCKS + SKEL]
    out[2], out[3] = row[1], sides[d, SIDE_BLOCKS + 2 * SKEL : SIDE_BLOCKS + 3 * SKEL]
    for a in range(3):
        out[4 + a] = row[2 + a]


def first_kernel(got, boxes, base, couple, part):
    part[...] = base[...] - dot(around(Here(), got, boxes), couple[...])


def put_together(here, kept, sides, row, whole):
    d = 1 - here.c
    mine, theirs = here.h * HALF, (1 - here.h) * HALF

    def put(number, offset, size, value):
        whole[pl.ds(pl.multiple_of(number * SKEL + offset, size), size)] = value

    def side(block, start, size):
        at = SIDE_BLOCKS + block * SKEL + start
        return sides[d, at : at + size]

    put(SOLVE_OWN, mine, HALF, kept[SOLVE_TWO : SOLVE_TWO + HALF])
    put(SOLVE_OWN, theirs, HALF, row[0, :HALF])
    put(SOLVE_SIDE, mine, HALF, side(0, 0, HALF))
    put(SOLVE_SIDE, theirs, HALF, row[1, :HALF])
    for a in range(3):
        for number, at, start in ((COUPLE_FAR, COUPLE_TWO, 0), (SPREAD_FAR, SPREAD_TWO, HALF)):
            at = at + (2 * a + 1) * HALF
            put(number + a, mine, HALF, kept[at : at + HALF])
            put(number + a, theirs, HALF, row[4 + a, start : start + HALF])
    own_at = (
        SOLVE_THREE,
        TOP_THREE,
        COUPLE_THREE + QUARTER,
        COUPLE_THREE + 2 * QUARTER,
        SPREAD_THREE + QUARTER,
        SPREAD_THREE + 2 * QUARTER,
    )
    for i in range(6):
        start = HALF + i * QUARTER if i < 2 else (i - 2) * QUARTER
        inverse = i < 2
        for c, h, value in (
            (here.c, here.h, kept[own_at[i] : own_at[i] + QUARTER]),
            (d, here.h, side(0 if inverse else 1, start, QUARTER)),
            (here.c, 1 - here.h, row[0 if inverse else 2, start : start + QUARTER]),
            (d, 1 - here.h, row[1 if inverse else 3, start : start + QUARTER]),
        ):
            put(SOLVE_ALL + i, (2 * c + h) * QUARTER, QUARTER, value)
    whole[ORDER_SIDE * SKEL :] = sides[d, SIDE_NUMBERS:]


def second_kernel(sums, kept, sides, row, chunk, base, zone, whole):
    here = Here()
    put_together(here, kept, sides, row, whole)
    c, d = here.c, 1 - here.c

    picked = pick(here.by_row(sums[c, c], sums[d, c]), numbers_of(kept, NUMBERS + ORDER_TWO))
    redund = picked[:, SKEL:]
    values = dot_t(redund, block_of(whole, SOLVE_OWN))
    zone[...] = values
    other = pick(here.by_row(sums[d, d], sums[c, d]), numbers_of(whole, ORDER_SIDE * SKEL + ORDER_TWO))
    other = dot_t(other[:, SKEL:], block_of(whole, SOLVE_SIDE))
    for slot in range(4):
        chunk[slot, 0] = values
        chunk[slot, 1] = other
    interp = kept[INTERP_TWO : INTERP_TWO + HALF]
    gone = dot_t(redund, stacked(interp, interp))
    base[...] = jnp.where(here.own_half(), picked[:, :SKEL] - gone, 0.0)


def second_part_kernel(near_at, far_at, got, chunk, base, kept, whole, part):
    here = Here()
    out_x, out_y, out_xy = here.outside(got, (0,))
    out_side = jnp.where(here.edge_y, 0.0, got[here.across, 1])
    near = jnp.zeros(VALUES, jnp.float32)
    far = jnp.zeros(VALUES, jnp.float32)
    for a, value, beyond in ((0, chunk[0, 1], out_side), (1, chunk[0, 0], out_y), (2, out_x, out_xy)):
        own = kept[near_at + 2 * a * HALF : near_at + (2 * a + 1) * HALF]
        near = near + dot_t(value, stacked(own, own))
        far = far + dot_t(beyond, block_of(whole, far_at + a))
    part[...] = base[...] - jnp.where(here.own_half(), near, 0.0) - far


def third_kernel(sums, kept, whole, chunk, base, zone):
    here = Here()
    joined = lanes(sums[0, 0] + sums[1, 0], sums[0, 1] + sums[1, 1])
    picked = pick(joined, numbers_of(kept, NUMBERS + ORDER_THREE))
    redund = picked[:, SKEL:]
    values = dot_t(redund, block_of(whole, SOLVE_ALL))
    zone[...] = values
    for slot in range(4):
        chunk[slot] = values
    gone = dot_t(redund, four(kept[INTERP_THREE : INTERP_THREE + QUARTER]))
    gone = gone + dot_t(values, four(kept[COUPLE_THREE : COUPLE_THREE + QUARTER]))
    base[...] = jnp.where(here.own_quarter(), picked[:, :SKEL] - gone, 0.0)


def third_part_kernel(at, got, base, whole, part):
    here = Here(crossed=True)
    out_x, out_y, out_xy = here.outside(got)
    edge = jnp.where(here.same, out_x, out_y)
    part[...] = base[...] - (dot_t(out_xy, block_of(whole, at)) + dot_t(edge, block_of(whole, at + 1)))


def total(sums):
    return (sums[0, 0] + sums[0, 1]) + (sums[1, 0] + sums[1, 1])


def top_kernel(sums, kept, whole, zone, chunk, base):
    here = Here()
    values = dot_t(total(sums), block_of(whole, TOP_ALL))
    for slot in range(4):
        chunk[slot] = values
    gone = dot_t(values, four(kept[SPREAD_THREE : SPREAD_THREE + QUARTER]))
    base[...] = jnp.where(here.own_quarter(), zone[...] - gone, 0.0)


def back_three_kernel(sums, values, kept, zone, chunk, base):
    here = Here()
    final = place(lanes(values[0], total(sums)), numbers_of(kept, NUMBERS + ORDER_THREE))
    low, high = final[:, :SKEL], final[:, SKEL:]
    own = jnp.where(here.c == 0, low, high)
    other = jnp.where(here.c == 0, high, low)
    for slot in range(4):
        chunk[slot, 0] = own
        chunk[slot, 1] = other
    base[...] = jnp.where(here.own_half(), zone[...], 0.0)


def back_two_kernel(sums, values, kept, whole, chunk, boxes):
    here = Here()
    c, d = here.c, 1 - here.c
    own = lanes(values[0, 0], sums[0, c] + sums[1, c])
    own = place(own, numbers_of(kept, NUMBERS + ORDER_TWO))
    other = lanes(values[0, 1], sums[0, d] + sums[1, d])
    other = place(other, numbers_of(whole, ORDER_SIDE * SKEL + ORDER_TWO))

    def rows_of(final):
        low, high = final[:, :SKEL], final[:, SKEL:]
        return jnp.where(here.h == 0, low, high), jnp.where(here.h == 0, high, low)

    value, value_row = rows_of(own)
    value_side, value_diag = rows_of(other)
    boxes[0], boxes[1], boxes[2], boxes[3] = value, value_side, value_row, value_diag
    fill(here, boxes, chunk)


def last_kernel(got, boxes, kept, adjoint, shares):
    here = Here()
    rest = kept[ZONE_ONE:] - dot(around(here, got, boxes), kept[LIFT_ONE : LIFT_ONE + 9 * SKEL])
    final = place(lanes(boxes[0], rest), numbers_of(kept, NUMBERS + ORDER_ONE))
    result = lanes(dot(final, kept[LEAF : LEAF + BOX]), dot(final, kept[LEAF + BOX : LEAF + 2 * BOX]))
    adjoint[...] = result
    field = lanes(kept[FIELD : FIELD + COLS], kept[FIELD + COLS : FIELD + 2 * COLS])
    count = lax.axis_size("rhs")
    weight = jnp.sum(result * field, axis=0, keepdims=True) / (count * COLS)
    share = PANELS // count
    number = lax.broadcasted_iota(jnp.int32, (8 * count, BOX), 0)
    panel = jnp.where(number % 8 < share, number // 8 * share + number % 8, -1)
    inside = numbers_of(kept, NUMBERS + PANEL_OF) == panel
    sums = jnp.sum(jnp.where(inside, weight, 0.0), axis=1, keepdims=True)
    for r in range(count):
        shares[r] = jnp.broadcast_to(sums[8 * r : 8 * (r + 1)], (8, SKEL))


def spec(space, count):
    return [pl.BlockSpec(memory_space=space)] * count


def call(body, outs, *operands):
    outs = tuple(pltpu.VMEM(shape, jnp.float32) for shape in outs)
    result = pl.pallas_call(
        body,
        out_shape=outs,
        in_specs=spec(pltpu.VMEM, len(operands)),
        out_specs=tuple(spec(pltpu.VMEM, len(outs))),
        compiler_params=pltpu.CompilerParams(vmem_limit_bytes=VMEM_LIMIT),
    )(*[pltpu.with_memory_space_constraint(operand, pltpu.VMEM) for operand in operands])
    return result if len(outs) > 1 else result[0]


def start(arrays):
    outs = [
        pltpu.VMEM(shape, jnp.float32)
        for shape in (VALUES, VALUES, (5, *BLOCK), (3 * SKEL + 8, SKEL), (9 * SKEL, SKEL), KEPT)
    ]
    return pl.pallas_call(
        start_kernel,
        out_shape=tuple(outs),
        in_specs=spec(pl.ANY, len(NAMES)),
        out_specs=tuple(spec(pltpu.VMEM, len(outs))),
        scratch_shapes=[pltpu.VMEM(arrays[name].shape, arrays[name].dtype) for name in NAMES]
        + [pltpu.SemaphoreType.DMA((len(NAMES),))],
        compiler_params=pltpu.CompilerParams(vmem_limit_bytes=VMEM_LIMIT),
    )(*[pltpu.with_memory_space_constraint(arrays[name], pltpu.HBM) for name in NAMES])


def on_device(groups, *arguments):
    arrays = {}
    for name, value in zip(GIVEN, arguments):
        value = value[0] if value.ndim == 3 else value[0, 0]
        if value.shape[-1] in (HALF, QUARTER):
            value = jnp.swapaxes(value, -1, -2)
        arrays[name] = value

    def outside(chunk, crossed=False):
        members = groups.crossed if crossed else groups.shifted
        return lax.all_to_all(chunk, AXES, 0, 0, axis_index_groups=members)

    def shared(part):
        pair = lax.all_gather(part, AXES, axis_index_groups=groups.diagonal)
        return lax.all_gather(pair, AXES, axis_index_groups=groups.sibling)

    def from_row(blocks):
        return lax.ppermute(blocks, "by", [(i, i ^ 1) for i in range(lax.axis_size("by"))])

    zone_one, base, to_row, to_side, couple, kept = start(arrays)
    pair = lax.all_gather(zone_one, AXES, axis_index_groups=groups.diagonal)
    to_side = call(side_kernel, [SIDE], pair, to_side)
    sides = lax.all_gather(to_side, AXES, axis_index_groups=groups.sibling)
    chunk, boxes, to_row = call(
        row_kernel, [(4, 2, *VALUES), (4, *VALUES), (7, *BLOCK)], to_row, sides
    )
    row = from_row(to_row)
    part = call(first_kernel, [VALUES], outside(chunk), boxes, base, couple)

    one, two, three = [(4, *VALUES), VALUES, VALUES], [(4, 2, *VALUES), VALUES, VALUES], [VALUES]
    chunk, base, zone_two, whole = call(second_kernel, two + [WHOLE], shared(part), kept, sides, row)
    down_two = functools.partial(second_part_kernel, COUPLE_TWO, COUPLE_FAR)
    part = call(down_two, three, outside(chunk), chunk, base, kept, whole)
    chunk, base, zone_three = call(third_kernel, one, shared(part), kept, whole)
    down_three = functools.partial(third_part_kernel, COUPLE_ALL)
    part = call(down_three, three, outside(chunk, True), base, whole)
    chunk, base = call(top_kernel, one[:2], shared(part), kept, whole, zone_three)
    up_three = functools.partial(third_part_kernel, SPREAD_ALL)
    part = call(up_three, three, outside(chunk, True), base, whole)
    chunk, base = call(back_three_kernel, two[:2], shared(part), chunk, kept, zone_two)
    up_two = functools.partial(second_part_kernel, SPREAD_TWO, SPREAD_FAR)
    part = call(up_two, three, outside(chunk), chunk, base, kept, whole)
    chunk, boxes = call(back_two_kernel, [(4, 2, *VALUES), (4, *VALUES)], shared(part), chunk, kept, whole)
    count = lax.axis_size("rhs")
    adjoint, shares = call(last_kernel, [(COLS, BOX), (count, 8, SKEL)], outside(chunk), boxes, kept)
    shares = lax.all_to_all(shares, "rhs", 0, 0)
    gradient = jnp.sum(shares[:, : PANELS // count, 0], axis=0)
    return adjoint[None, None], gradient[None, None]


def solution(mesh):
    box = P("bx", "by")
    columns = P("bx", "by", "rhs", None)
    groups = Groups(mesh.shape["bx"], mesh.shape["by"], mesh.shape["rhs"])
    return jax.shard_map(
        functools.partial(on_device, groups),
        mesh=mesh,
        in_specs=(columns, columns) + (box,) * 23,
        out_specs=(columns, P("bx", "by", "rhs")),
        check_vma=False,
    )
```

```python
import functools

import jax
import jax.numpy as jnp
from jax import lax
from jax.experimental import pallas as pl
from jax.experimental.pallas import tpu as pltpu
from jax.sharding import PartitionSpec as P

PANELS = 16
SKEL = 128
HALF = SKEL // 2
QUARTER = SKEL // 4
BOX = 2 * SKEL
COLS = 16
VMEM_LIMIT = 8 << 20
AXES = ("bx", "by", "rhs")
VALUES = (COLS, SKEL)
BLOCK = (SKEL, SKEL)


def halves(values):
    high = values.astype(jnp.bfloat16)
    low = (values - high.astype(jnp.float32)).astype(jnp.bfloat16)
    return high, low


def dims(left, rights, contract):
    left = jnp.concatenate(halves(left), axis=0)
    size = left.shape[0] // 2
    result = None
    for right in rights:
        product = lax.dot_general(
            left, right, (((1,), (contract,)), ((), ())), preferred_element_type=jnp.float32
        )
        product = product[:size] + product[size:]
        result = product if result is None else result + product
    return result


def dot(left, right):
    return dims(left, halves(right), 0)


def dot_t(left, right):
    return dims(left, halves(right), 1)


def pick(values, order):
    return dims(values, (chosen(order),), 0)


def place(values, order):
    return dims(values, (chosen(order),), 1)


def lanes(*parts):
    return jnp.concatenate(parts, axis=1)


def stacked(*parts):
    return jnp.concatenate(parts, axis=0)


class Groups:
    def __init__(self, size_x, size_y, size_r):
        def place(i, j, r):
            return (i * size_y + j) * size_r + r

        every = [(i, j, r) for i in range(size_x) for j in range(size_y) for r in range(size_r)]
        self.sibling = [[place(i, j, r), place(i + 1, j, r)] for i, j, r in every if i % 2 == 0]
        self.diagonal = [[place(i, j, r), place(i + 1, j ^ 1, r)] for i, j, r in every if i % 2 == 0]
        self.shifted, self.crossed = [], []
        last = size_x - 1
        for j in range(1, size_y, 2):
            for r in range(size_r):
                for i in range(1, last, 2):
                    shifted, crossed = [(i, j), (i + 1, j)], [(i, j), (i + 1, j)]
                    if j + 1 < size_y:
                        shifted += [(i, j + 1), (i + 1, j + 1)]
                        crossed += [(i - 1, j + 1), (i + 2, j + 1)]
                        self.shifted.append([place(*at, r) for at in shifted])
                        self.crossed.append([place(*at, r) for at in crossed])
                    elif r % 2 == 0:
                        low = [(i, 0), (i + 1, 0)], [(i - 1, 0), (i + 2, 0)]
                        for groups, members in (
                            (self.shifted, shifted),
                            (self.crossed, crossed),
                            (self.shifted, low[0]),
                            (self.crossed, low[1]),
                        ):
                            groups.append([place(*at, r + n) for n in (0, 1) for at in members])
                for i in (0, last):
                    for groups, k in ((self.shifted, i), (self.crossed, i ^ 1)):
                        if j + 1 < size_y and r % 2 == 0:
                            groups.append([place(*at, r + n) for at in ((i, j), (k, j + 1)) for n in (0, 1)])
                        elif j + 1 == size_y and r % 4 == 0:
                            groups.append([place(i, j, r + n) for n in range(4)])
                            groups.append([place(k, 0, r + n) for n in range(4)])


class Here:
    def __init__(self, crossed=False):
        x, y, r = (lax.axis_index(axis) for axis in AXES)
        self.c, self.h = lax.rem(x, 2), lax.rem(y, 2)
        side = jnp.where(self.h == 0, 1 - self.c, self.c) if crossed else self.c
        chip = x - self.c
        self.edge_x = ((chip == 0) & (side == 0)) | ((chip == lax.axis_size("bx") - 2) & (side == 1))
        self.edge_y = (y == 0) | (y == lax.axis_size("by") - 1)
        slot_x = jnp.where(self.edge_x, lax.rem(r, 2), 1 - side)
        shared = jnp.where(self.edge_x, lax.rem(r, 4) // 2, lax.rem(r, 2))
        slot_y = jnp.where(self.edge_y, shared, 1 - self.h)
        self.slot_y = slot_y
        self.along = 2 * slot_y + 1 - slot_x
        self.across = 2 * (1 - slot_y) + slot_x
        self.corner = 2 * (1 - slot_y) + 1 - slot_x
        side_x = (2 - 2 * side, 1, 2 * side)
        side_y = (2 - 2 * self.h, 1, 2 * self.h)
        self.block = [[3 * a + b for b in side_y] for a in side_x]
        self.same = side == self.h

    def outside(self, got, item=()):
        x = jnp.where(self.edge_x, 0.0, got[(self.along, *item)])
        y = jnp.where(self.edge_y, 0.0, got[(self.across, *item)])
        xy = jnp.where(self.edge_x | self.edge_y, 0.0, got[(self.corner, *item)])
        return x, y, xy

    def by_row(self, own, other):
        return lanes(jnp.where(self.h == 0, own, other), jnp.where(self.h == 0, other, own))

    def own_half(self):
        lane = lax.broadcasted_iota(jnp.int32, VALUES, 1)
        return lane // HALF == self.h

    def own_quarter(self):
        lane = lax.broadcasted_iota(jnp.int32, VALUES, 1)
        return lane // QUARTER == 2 * self.c + self.h


def chosen(order):
    found = lax.broadcasted_iota(jnp.int32, (BOX, BOX), 0) == order
    return jnp.where(found, 1.0, 0.0).astype(jnp.bfloat16)


def four(values):
    return stacked(values, values, values, values)


NAMES = (
    "rhs_nodes",
    "leaf_map",
    "order_one",
    "solve_one",
    "interp_one",
    "near_one",
    "couple_one",
    "spread_one",
    "couple_two",
    "spread_two",
    "couple_three",
    "spread_three",
    "solve_two",
    "solve_three",
    "top_three",
    "interp_two",
    "interp_three",
    "back_one",
    "back_two",
    "back_three",
    "order_two",
    "order_three",
    "node_panel",
    "forward",
    "derivative",
)
GIVEN = (
    "rhs_nodes",
    "forward",
    "leaf_map",
    "derivative",
    "node_panel",
    "order_one",
    "near_one",
    "interp_one",
    "solve_one",
    "couple_one",
    "back_one",
    "spread_one",
    "order_two",
    "interp_two",
    "solve_two",
    "couple_two",
    "back_two",
    "spread_two",
    "order_three",
    "interp_three",
    "solve_three",
    "couple_three",
    "back_three",
    "spread_three",
    "top_three",
)

LIFT_ONE = 0
LEAF = LIFT_ONE + 9 * SKEL
COUPLE_TWO = LEAF + 2 * BOX
SPREAD_TWO = COUPLE_TWO + 6 * HALF
INTERP_TWO = SPREAD_TWO + 6 * HALF
SOLVE_TWO = INTERP_TWO + HALF
COUPLE_THREE = SOLVE_TWO + HALF
SPREAD_THREE = COUPLE_THREE + 3 * QUARTER
INTERP_THREE = SPREAD_THREE + 3 * QUARTER
SOLVE_THREE = INTERP_THREE + QUARTER
TOP_THREE = SOLVE_THREE + QUARTER
NUMBERS = TOP_THREE + QUARTER
FIELD = NUMBERS + 8
ZONE_ONE = FIELD + 2 * COLS
KEPT = (ZONE_ONE + COLS, SKEL)
ORDER_ONE, ORDER_TWO, ORDER_THREE, PANEL_OF = range(0, 8, 2)

SOLVE_OWN, SOLVE_SIDE, SOLVE_ALL, TOP_ALL, COUPLE_ALL, SPREAD_ALL = 0, 1, 2, 3, 4, 6
COUPLE_FAR, SPREAD_FAR, ORDER_SIDE = 8, 11, 14
WHOLE = (ORDER_SIDE * SKEL + 8, SKEL)
SIDE_BLOCKS = 2 * COLS
SIDE_NUMBERS = SIDE_BLOCKS + 3 * SKEL
SIDE = (SIDE_NUMBERS + 8, SKEL)


def numbers_of(ref, row):
    return lanes(ref[row : row + 1], ref[row + 1 : row + 2]).astype(jnp.int32)


def block_of(ref, number):
    return ref[number * SKEL : (number + 1) * SKEL]


def start_kernel(*refs):
    count = len(NAMES)
    source = dict(zip(NAMES, refs[:count]))
    zone, base, row_out, side_out, couple, kept = refs[count : count + 6]
    held = dict(zip(NAMES, refs[count + 6 : -1]))
    sems = refs[-1]
    here = Here()
    copies = {name: pltpu.make_async_copy(source[name], held[name], sems.at[i]) for i, name in enumerate(NAMES)}
    for name in NAMES:
        copies[name].start()

    def read(name):
        copies[name].wait()
        return held[name][...]

    rhs, leaf = read("rhs_nodes"), read("leaf_map")
    candidates = dot_t(rhs, leaf)
    kept[LEAF : LEAF + BOX] = leaf[:, :SKEL]
    kept[LEAF + BOX : LEAF + 2 * BOX] = leaf[:, SKEL:]
    picked = pick(candidates, read("order_one"))
    redund = picked[:, SKEL:]
    values = dot(redund, read("solve_one"))
    zone[...] = values
    kept[ZONE_ONE:] = values
    base[...] = picked[:, :SKEL] - dot(redund, read("interp_one"))
    spots = lax.broadcasted_iota(jnp.int32, (16, 9), 0) == lax.broadcasted_iota(jnp.int32, (16, 9), 1)
    near = jnp.where(spots, read("near_one").astype(jnp.float32), 0.0)
    near = jnp.broadcast_to(jnp.sum(near, axis=1, keepdims=True), VALUES)
    number = lax.broadcasted_iota(jnp.int32, VALUES, 0)

    def scaled(name, a, b):
        n = here.block[a][b]
        weight = jnp.sum(jnp.where(number == n, near, 0.0), axis=0, keepdims=True)
        return weight * held[name][n]

    for name in NAMES[NAMES.index("couple_one") :]:
        copies[name].wait()
    for out, start in ((row_out.at[0], 0), (side_out, 0)):
        out[start : start + HALF] = held["solve_two"][...]
        out[start + HALF : start + HALF + QUARTER] = held["solve_three"][...]
        out[start + HALF + QUARTER : start + SKEL] = held["top_three"][...]
    cross = Here(crossed=True)

    def third(out, start, corner, edge_same, edge_else):
        corner = cross.block[corner[0]][corner[1]]
        edge = jnp.where(
            cross.same, cross.block[edge_same[0]][edge_same[1]], cross.block[edge_else[0]][edge_else[1]]
        )
        for i, (name, n) in enumerate(
            (("couple_three", corner), ("couple_three", edge), ("spread_three", corner), ("spread_three", edge))
        ):
            out[start + i * QUARTER : start + (i + 1) * QUARTER] = held[name][n]

    third(row_out.at[1], 0, (0, 0), (0, 1), (1, 0))
    third(side_out, SKEL, (0, 2), (1, 2), (0, 1))
    third(side_out, 2 * SKEL, (2, 0), (1, 0), (2, 1))
    for a in range(3):
        n = here.block[a][0]
        row_out[2 + a, :HALF] = held["couple_two"][n]
        row_out[2 + a, HALF:] = held["spread_two"][n]
    for a in range(3):
        for b in range(3):
            at = (3 * a + b) * SKEL
            couple[at : at + SKEL] = scaled("couple_one", a, b)
            at = LIFT_ONE + at
            block = scaled("spread_one", a, b)
            kept[at : at + SKEL] = block + held["back_one"][...] if a == b == 1 else block
        for b in (1, 2):
            n = here.block[a][b]
            at = COUPLE_TWO + (2 * a + b - 1) * HALF
            kept[at : at + HALF] = held["couple_two"][n]
            at = SPREAD_TWO + (2 * a + b - 1) * HALF
            block = held["spread_two"][n]
            kept[at : at + HALF] = block + held["back_two"][...] if a == b == 1 else block
    edge = jnp.where(cross.same, cross.block[2][1], cross.block[1][2])
    for i, n in enumerate((4, cross.block[2][2], edge)):
        at = COUPLE_THREE + i * QUARTER
        kept[at : at + QUARTER] = held["couple_three"][n]
        at = SPREAD_THREE + i * QUARTER
        block = held["spread_three"][n]
        kept[at : at + QUARTER] = block + held["back_three"][...] if i == 0 else block
    for name, at in (
        ("interp_two", INTERP_TWO),
        ("solve_two", SOLVE_TWO),
        ("interp_three", INTERP_THREE),
        ("solve_three", SOLVE_THREE),
        ("top_three", TOP_THREE),
    ):
        kept[at : at + held[name].shape[0]] = held[name][...]
    for name, row in (
        ("order_one", ORDER_ONE),
        ("order_two", ORDER_TWO),
        ("order_three", ORDER_THREE),
        ("node_panel", PANEL_OF),
    ):
        numbers = held[name][...].astype(jnp.float32)
        kept[NUMBERS + row : NUMBERS + row + 1] = numbers[:, :SKEL]
        kept[NUMBERS + row + 1 : NUMBERS + row + 2] = numbers[:, SKEL:]
    side_out[3 * SKEL :] = kept[NUMBERS : NUMBERS + 8]
    field = dot(held["forward"][...], held["derivative"][...])
    kept[FIELD : FIELD + COLS] = field[:, :SKEL]
    kept[FIELD + COLS : FIELD + 2 * COLS] = field[:, SKEL:]


def side_kernel(pair, side, out):
    out[:COLS], out[COLS:SIDE_BLOCKS] = pair[0], pair[1]
    out[SIDE_BLOCKS:] = side[...]


def fill(here, boxes, chunk):
    for slot in range(4):
        chunk[slot, 0] = boxes[0]
        chunk[slot, 1] = jnp.where(here.slot_y == slot // 2, boxes[2], boxes[1])


def around(here, got, boxes):
    out_x, out_y, out_xy = here.outside(got, (0,))
    out_x_row = jnp.where(here.edge_x, 0.0, got[here.along, 1])
    out_y_side = jnp.where(here.edge_y, 0.0, got[here.across, 1])
    return lanes(boxes[3], boxes[1], out_y_side, boxes[2], boxes[0], out_y, out_x_row, out_x, out_xy)


def row_kernel(row, sides, chunk, boxes, out):
    here = Here()
    c, d = here.c, 1 - here.c
    for box, (member, number) in enumerate(((c, c), (d, d), (d, c), (c, d))):
        boxes[box] = sides[member, pl.ds(pl.multiple_of(number * COLS, COLS), COLS)]
    fill(here, boxes, chunk)
    out[0], out[1] = row[0], sides[d, SIDE_BLOCKS : SIDE_BLOCKS + SKEL]
    out[2], out[3] = row[1], sides[d, SIDE_BLOCKS + 2 * SKEL : SIDE_BLOCKS + 3 * SKEL]
    for a in range(3):
        out[4 + a] = row[2 + a]


def first_kernel(got, boxes, base, couple, part):
    part[...] = base[...] - dot(around(Here(), got, boxes), couple[...])


def put_together(here, kept, sides, row, whole):
    d = 1 - here.c
    mine, theirs = here.h * HALF, (1 - here.h) * HALF

    def put(number, offset, size, value):
        whole[pl.ds(pl.multiple_of(number * SKEL + offset, size), size)] = value

    def side(block, start, size):
        at = SIDE_BLOCKS + block * SKEL + start
        return sides[d, at : at + size]

    put(SOLVE_OWN, mine, HALF, kept[SOLVE_TWO : SOLVE_TWO + HALF])
    put(SOLVE_OWN, theirs, HALF, row[0, :HALF])
    put(SOLVE_SIDE, mine, HALF, side(0, 0, HALF))
    put(SOLVE_SIDE, theirs, HALF, row[1, :HALF])
    for a in range(3):
        for number, at, start in ((COUPLE_FAR, COUPLE_TWO, 0), (SPREAD_FAR, SPREAD_TWO, HALF)):
            at = at + (2 * a + 1) * HALF
            put(number + a, mine, HALF, kept[at : at + HALF])
            put(number + a, theirs, HALF, row[4 + a, start : start + HALF])
    own_at = (
        SOLVE_THREE,
        TOP_THREE,
        COUPLE_THREE + QUARTER,
        COUPLE_THREE + 2 * QUARTER,
        SPREAD_THREE + QUARTER,
        SPREAD_THREE + 2 * QUARTER,
    )
    for i in range(6):
        start = HALF + i * QUARTER if i < 2 else (i - 2) * QUARTER
        inverse = i < 2
        for c, h, value in (
            (here.c, here.h, kept[own_at[i] : own_at[i] + QUARTER]),
            (d, here.h, side(0 if inverse else 1, start, QUARTER)),
            (here.c, 1 - here.h, row[0 if inverse else 2, start : start + QUARTER]),
            (d, 1 - here.h, row[1 if inverse else 3, start : start + QUARTER]),
        ):
            put(SOLVE_ALL + i, (2 * c + h) * QUARTER, QUARTER, value)
    whole[ORDER_SIDE * SKEL :] = sides[d, SIDE_NUMBERS:]


def second_kernel(sums, kept, sides, row, chunk, base, zone, whole):
    here = Here()
    put_together(here, kept, sides, row, whole)
    c, d = here.c, 1 - here.c

    picked = pick(here.by_row(sums[c, c], sums[d, c]), numbers_of(kept, NUMBERS + ORDER_TWO))
    redund = picked[:, SKEL:]
    values = dot_t(redund, block_of(whole, SOLVE_OWN))
    zone[...] = values
    other = pick(here.by_row(sums[d, d], sums[c, d]), numbers_of(whole, ORDER_SIDE * SKEL + ORDER_TWO))
    other = dot_t(other[:, SKEL:], block_of(whole, SOLVE_SIDE))
    for slot in range(4):
        chunk[slot, 0] = values
        chunk[slot, 1] = other
    interp = kept[INTERP_TWO : INTERP_TWO + HALF]
    gone = dot_t(redund, stacked(interp, interp))
    base[...] = jnp.where(here.own_half(), picked[:, :SKEL] - gone, 0.0)


def second_part_kernel(near_at, far_at, got, chunk, base, kept, whole, part):
    here = Here()
    out_x, out_y, out_xy = here.outside(got, (0,))
    out_side = jnp.where(here.edge_y, 0.0, got[here.across, 1])
    near = jnp.zeros(VALUES, jnp.float32)
    far = jnp.zeros(VALUES, jnp.float32)
    for a, value, beyond in ((0, chunk[0, 1], out_side), (1, chunk[0, 0], out_y), (2, out_x, out_xy)):
        own = kept[near_at + 2 * a * HALF : near_at + (2 * a + 1) * HALF]
        near = near + dot_t(value, stacked(own, own))
        far = far + dot_t(beyond, block_of(whole, far_at + a))
    part[...] = base[...] - jnp.where(here.own_half(), near, 0.0) - far


def third_kernel(sums, kept, whole, chunk, base, zone):
    here = Here()
    joined = lanes(sums[0, 0] + sums[1, 0], sums[0, 1] + sums[1, 1])
    picked = pick(joined, numbers_of(kept, NUMBERS + ORDER_THREE))
    redund = picked[:, SKEL:]
    values = dot_t(redund, block_of(whole, SOLVE_ALL))
    zone[...] = values
    for slot in range(4):
        chunk[slot] = values
    gone = dot_t(redund, four(kept[INTERP_THREE : INTERP_THREE + QUARTER]))
    gone = gone + dot_t(values, four(kept[COUPLE_THREE : COUPLE_THREE + QUARTER]))
    base[...] = jnp.where(here.own_quarter(), picked[:, :SKEL] - gone, 0.0)


def third_part_kernel(at, got, base, whole, part):
    here = Here(crossed=True)
    out_x, out_y, out_xy = here.outside(got)
    edge = jnp.where(here.same, out_x, out_y)
    part[...] = base[...] - (dot_t(out_xy, block_of(whole, at)) + dot_t(edge, block_of(whole, at + 1)))


def total(sums):
    return (sums[0, 0] + sums[0, 1]) + (sums[1, 0] + sums[1, 1])


def top_kernel(sums, kept, whole, zone, chunk, base):
    here = Here()
    values = dot_t(total(sums), block_of(whole, TOP_ALL))
    for slot in range(4):
        chunk[slot] = values
    gone = dot_t(values, four(kept[SPREAD_THREE : SPREAD_THREE + QUARTER]))
    base[...] = jnp.where(here.own_quarter(), zone[...] - gone, 0.0)


def back_three_kernel(sums, values, kept, zone, chunk, base):
    here = Here()
    final = place(lanes(values[0], total(sums)), numbers_of(kept, NUMBERS + ORDER_THREE))
    low, high = final[:, :SKEL], final[:, SKEL:]
    own = jnp.where(here.c == 0, low, high)
    other = jnp.where(here.c == 0, high, low)
    for slot in range(4):
        chunk[slot, 0] = own
        chunk[slot, 1] = other
    base[...] = jnp.where(here.own_half(), zone[...], 0.0)


def back_two_kernel(sums, values, kept, whole, chunk, boxes):
    here = Here()
    c, d = here.c, 1 - here.c
    own = lanes(values[0, 0], sums[0, c] + sums[1, c])
    own = place(own, numbers_of(kept, NUMBERS + ORDER_TWO))
    other = lanes(values[0, 1], sums[0, d] + sums[1, d])
    other = place(other, numbers_of(whole, ORDER_SIDE * SKEL + ORDER_TWO))

    def rows_of(final):
        low, high = final[:, :SKEL], final[:, SKEL:]
        return jnp.where(here.h == 0, low, high), jnp.where(here.h == 0, high, low)

    value, value_row = rows_of(own)
    value_side, value_diag = rows_of(other)
    boxes[0], boxes[1], boxes[2], boxes[3] = value, value_side, value_row, value_diag
    fill(here, boxes, chunk)


def last_kernel(got, boxes, kept, adjoint, shares):
    here = Here()
    rest = kept[ZONE_ONE:] - dot(around(here, got, boxes), kept[LIFT_ONE : LIFT_ONE + 9 * SKEL])
    final = place(lanes(boxes[0], rest), numbers_of(kept, NUMBERS + ORDER_ONE))
    result = lanes(dot(final, kept[LEAF : LEAF + BOX]), dot(final, kept[LEAF + BOX : LEAF + 2 * BOX]))
    adjoint[...] = result
    field = lanes(kept[FIELD : FIELD + COLS], kept[FIELD + COLS : FIELD + 2 * COLS])
    count = lax.axis_size("rhs")
    weight = jnp.sum(result * field, axis=0, keepdims=True) / (count * COLS)
    share = PANELS // count
    number = lax.broadcasted_iota(jnp.int32, (SKEL, BOX), 0)
    panels = numbers_of(kept, NUMBERS + PANEL_OF)
    weight = jnp.broadcast_to(weight, (COLS, BOX))
    for r in range(count):
        inside = (number < share) & (panels == number + r * share)
        inside = jnp.where(inside, 1.0, 0.0).astype(jnp.bfloat16)
        shares[r] = dims(weight, (inside,), 1)[:8]


def end_kernel(adjoint, shares, adjoint_out, gradient_out):
    adjoint_out[...] = adjoint[...]
    total = shares[0, 0:1] + shares[1, 0:1]
    for r in range(2, shares.shape[0]):
        total = total + shares[r, 0:1]
    gradient_out[...] = total[:, : gradient_out.shape[1]]


def spec(space, count):
    return [pl.BlockSpec(memory_space=space)] * count


def call(body, outs, *operands):
    outs = tuple(pltpu.VMEM(shape, jnp.float32) for shape in outs)
    result = pl.pallas_call(
        body,
        out_shape=outs,
        in_specs=spec(pltpu.VMEM, len(operands)),
        out_specs=tuple(spec(pltpu.VMEM, len(outs))),
        compiler_params=pltpu.CompilerParams(vmem_limit_bytes=VMEM_LIMIT),
    )(*[pltpu.with_memory_space_constraint(operand, pltpu.VMEM) for operand in operands])
    return result if len(outs) > 1 else result[0]


def start(arrays):
    outs = [
        pltpu.VMEM(shape, jnp.float32)
        for shape in (VALUES, VALUES, (5, *BLOCK), (3 * SKEL + 8, SKEL), (9 * SKEL, SKEL), KEPT)
    ]
    return pl.pallas_call(
        start_kernel,
        out_shape=tuple(outs),
        in_specs=spec(pl.ANY, len(NAMES)),
        out_specs=tuple(spec(pltpu.VMEM, len(outs))),
        scratch_shapes=[pltpu.VMEM(arrays[name].shape, arrays[name].dtype) for name in NAMES]
        + [pltpu.SemaphoreType.DMA((len(NAMES),))],
        compiler_params=pltpu.CompilerParams(vmem_limit_bytes=VMEM_LIMIT),
    )(*[pltpu.with_memory_space_constraint(arrays[name], pltpu.HBM) for name in NAMES])


def on_device(groups, *arguments):
    arrays = {}
    for name, value in zip(GIVEN, arguments):
        value = value[0] if value.ndim == 3 else value[0, 0]
        if value.shape[-1] in (HALF, QUARTER):
            value = jnp.swapaxes(value, -1, -2)
        arrays[name] = value

    def outside(chunk, crossed=False):
        members = groups.crossed if crossed else groups.shifted
        return lax.all_to_all(chunk, AXES, 0, 0, axis_index_groups=members)

    def shared(part):
        pair = lax.all_gather(part, AXES, axis_index_groups=groups.diagonal)
        return lax.all_gather(pair, AXES, axis_index_groups=groups.sibling)

    def from_row(blocks):
        return lax.ppermute(blocks, "by", [(i, i ^ 1) for i in range(lax.axis_size("by"))])

    zone_one, base, to_row, to_side, couple, kept = start(arrays)
    pair = lax.all_gather(zone_one, AXES, axis_index_groups=groups.diagonal)
    to_side = call(side_kernel, [SIDE], pair, to_side)
    sides = lax.all_gather(to_side, AXES, axis_index_groups=groups.sibling)
    chunk, boxes, to_row = call(
        row_kernel, [(4, 2, *VALUES), (4, *VALUES), (7, *BLOCK)], to_row, sides
    )
    row = from_row(to_row)
    part = call(first_kernel, [VALUES], outside(chunk), boxes, base, couple)

    one, two, three = [(4, *VALUES), VALUES, VALUES], [(4, 2, *VALUES), VALUES, VALUES], [VALUES]
    chunk, base, zone_two, whole = call(second_kernel, two + [WHOLE], shared(part), kept, sides, row)
    down_two = functools.partial(second_part_kernel, COUPLE_TWO, COUPLE_FAR)
    part = call(down_two, three, outside(chunk), chunk, base, kept, whole)
    chunk, base, zone_three = call(third_kernel, one, shared(part), kept, whole)
    down_three = functools.partial(third_part_kernel, COUPLE_ALL)
    part = call(down_three, three, outside(chunk, True), base, whole)
    chunk, base = call(top_kernel, one[:2], shared(part), kept, whole, zone_three)
    up_three = functools.partial(third_part_kernel, SPREAD_ALL)
    part = call(up_three, three, outside(chunk, True), base, whole)
    chunk, base = call(back_three_kernel, two[:2], shared(part), chunk, kept, zone_two)
    up_two = functools.partial(second_part_kernel, SPREAD_TWO, SPREAD_FAR)
    part = call(up_two, three, outside(chunk), chunk, base, kept, whole)
    chunk, boxes = call(back_two_kernel, [(4, 2, *VALUES), (4, *VALUES)], shared(part), chunk, kept, whole)
    count = lax.axis_size("rhs")
    adjoint, shares = call(last_kernel, [(COLS, BOX), (count, 8, SKEL)], outside(chunk), boxes, kept)
    shares = lax.all_to_all(shares, "rhs", 0, 0)
    adjoint, gradient = pl.pallas_call(
        end_kernel,
        out_shape=(
            jax.ShapeDtypeStruct((COLS, BOX), jnp.float32),
            jax.ShapeDtypeStruct((1, PANELS // count), jnp.float32),
        ),
        in_specs=spec(pltpu.VMEM, 2),
        out_specs=tuple(spec(pltpu.VMEM, 2)),
        compiler_params=pltpu.CompilerParams(vmem_limit_bytes=VMEM_LIMIT),
    )(*[pltpu.with_memory_space_constraint(operand, pltpu.VMEM) for operand in (adjoint, shares)])
    return adjoint[None, None], gradient[None]


def solution(mesh):
    box = P("bx", "by")
    columns = P("bx", "by", "rhs", None)
    groups = Groups(mesh.shape["bx"], mesh.shape["by"], mesh.shape["rhs"])
    return jax.shard_map(
        functools.partial(on_device, groups),
        mesh=mesh,
        in_specs=(columns, columns) + (box,) * 23,
        out_specs=(columns, P("bx", "by", "rhs")),
        check_vma=False,
    )
```

```python
import functools

import jax
import jax.numpy as jnp
from jax import lax
from jax.experimental import pallas as pl
from jax.experimental.pallas import tpu as pltpu
from jax.sharding import PartitionSpec as P

PANELS = 16
SKEL = 128
HALF = SKEL // 2
QUARTER = SKEL // 4
BOX = 2 * SKEL
COLS = 16
VMEM_LIMIT = 8 << 20
AXES = ("bx", "by", "rhs")
VALUES = (COLS, SKEL)
BLOCK = (SKEL, SKEL)


def halves(values):
    high = values.astype(jnp.bfloat16)
    low = (values - high.astype(jnp.float32)).astype(jnp.bfloat16)
    return high, low


def dims(left, rights, contract):
    left = jnp.concatenate(halves(left), axis=0)
    size = left.shape[0] // 2
    result = None
    for right in rights:
        product = lax.dot_general(
            left, right, (((1,), (contract,)), ((), ())), preferred_element_type=jnp.float32
        )
        product = product[:size] + product[size:]
        result = product if result is None else result + product
    return result


def dot(left, right):
    return dims(left, halves(right), 0)


def dot_t(left, right):
    return dims(left, halves(right), 1)


def pick(values, order):
    return dims(values, (chosen(order),), 0)


def place(values, order):
    return dims(values, (chosen(order),), 1)


def lanes(*parts):
    return jnp.concatenate(parts, axis=1)


def stacked(*parts):
    return jnp.concatenate(parts, axis=0)


class Groups:
    def __init__(self, size_x, size_y, size_r):
        def place(i, j, r):
            return (i * size_y + j) * size_r + r

        every = [(i, j, r) for i in range(size_x) for j in range(size_y) for r in range(size_r)]
        self.sibling = [[place(i, j, r), place(i + 1, j, r)] for i, j, r in every if i % 2 == 0]
        self.diagonal = [[place(i, j, r), place(i + 1, j ^ 1, r)] for i, j, r in every if i % 2 == 0]
        self.shifted, self.crossed = [], []
        last = size_x - 1
        for j in range(1, size_y, 2):
            for r in range(size_r):
                for i in range(1, last, 2):
                    shifted, crossed = [(i, j), (i + 1, j)], [(i, j), (i + 1, j)]
                    if j + 1 < size_y:
                        shifted += [(i, j + 1), (i + 1, j + 1)]
                        crossed += [(i - 1, j + 1), (i + 2, j + 1)]
                        self.shifted.append([place(*at, r) for at in shifted])
                        self.crossed.append([place(*at, r) for at in crossed])
                    elif r % 2 == 0:
                        low = [(i, 0), (i + 1, 0)], [(i - 1, 0), (i + 2, 0)]
                        for groups, members in (
                            (self.shifted, shifted),
                            (self.crossed, crossed),
                            (self.shifted, low[0]),
                            (self.crossed, low[1]),
                        ):
                            groups.append([place(*at, r + n) for n in (0, 1) for at in members])
                for i in (0, last):
                    for groups, k in ((self.shifted, i), (self.crossed, i ^ 1)):
                        if j + 1 < size_y and r % 2 == 0:
                            groups.append([place(*at, r + n) for at in ((i, j), (k, j + 1)) for n in (0, 1)])
                        elif j + 1 == size_y and r % 4 == 0:
                            groups.append([place(i, j, r + n) for n in range(4)])
                            groups.append([place(k, 0, r + n) for n in range(4)])


class Here:
    def __init__(self, crossed=False):
        x, y, r = (lax.axis_index(axis) for axis in AXES)
        self.c, self.h = lax.rem(x, 2), lax.rem(y, 2)
        side = jnp.where(self.h == 0, 1 - self.c, self.c) if crossed else self.c
        chip = x - self.c
        self.edge_x = ((chip == 0) & (side == 0)) | ((chip == lax.axis_size("bx") - 2) & (side == 1))
        self.edge_y = (y == 0) | (y == lax.axis_size("by") - 1)
        slot_x = jnp.where(self.edge_x, lax.rem(r, 2), 1 - side)
        shared = jnp.where(self.edge_x, lax.rem(r, 4) // 2, lax.rem(r, 2))
        slot_y = jnp.where(self.edge_y, shared, 1 - self.h)
        self.slot_y = slot_y
        self.along = 2 * slot_y + 1 - slot_x
        self.across = 2 * (1 - slot_y) + slot_x
        self.corner = 2 * (1 - slot_y) + 1 - slot_x
        side_x = (2 - 2 * side, 1, 2 * side)
        side_y = (2 - 2 * self.h, 1, 2 * self.h)
        self.block = [[3 * a + b for b in side_y] for a in side_x]
        self.same = side == self.h

    def outside(self, got, item=()):
        x = jnp.where(self.edge_x, 0.0, got[(self.along, *item)])
        y = jnp.where(self.edge_y, 0.0, got[(self.across, *item)])
        xy = jnp.where(self.edge_x | self.edge_y, 0.0, got[(self.corner, *item)])
        return x, y, xy

    def by_row(self, own, other):
        return lanes(jnp.where(self.h == 0, own, other), jnp.where(self.h == 0, other, own))

    def own_half(self):
        lane = lax.broadcasted_iota(jnp.int32, VALUES, 1)
        return lane // HALF == self.h

    def own_quarter(self):
        lane = lax.broadcasted_iota(jnp.int32, VALUES, 1)
        return lane // QUARTER == 2 * self.c + self.h


def chosen(order):
    found = lax.broadcasted_iota(jnp.int32, (BOX, BOX), 0) == order
    return jnp.where(found, 1.0, 0.0).astype(jnp.bfloat16)


def four(values):
    return stacked(values, values, values, values)


NAMES = (
    "rhs_nodes",
    "leaf_map",
    "order_one",
    "solve_one",
    "interp_one",
    "near_one",
    "couple_two",
    "spread_two",
    "couple_three",
    "spread_three",
    "solve_two",
    "solve_three",
    "top_three",
    "interp_two",
    "interp_three",
    "back_one",
    "back_two",
    "back_three",
    "order_two",
    "order_three",
    "node_panel",
    "forward",
    "derivative",
)
GIVEN = (
    "rhs_nodes",
    "forward",
    "leaf_map",
    "derivative",
    "node_panel",
    "order_one",
    "near_one",
    "interp_one",
    "solve_one",
    "couple_one",
    "back_one",
    "spread_one",
    "order_two",
    "interp_two",
    "solve_two",
    "couple_two",
    "back_two",
    "spread_two",
    "order_three",
    "interp_three",
    "solve_three",
    "couple_three",
    "back_three",
    "spread_three",
    "top_three",
)

BACK_ONE = 0
LEAF = BACK_ONE + SKEL
COUPLE_TWO = LEAF + 2 * BOX
SPREAD_TWO = COUPLE_TWO + 6 * HALF
INTERP_TWO = SPREAD_TWO + 6 * HALF
SOLVE_TWO = INTERP_TWO + HALF
COUPLE_THREE = SOLVE_TWO + HALF
SPREAD_THREE = COUPLE_THREE + 3 * QUARTER
INTERP_THREE = SPREAD_THREE + 3 * QUARTER
SOLVE_THREE = INTERP_THREE + QUARTER
TOP_THREE = SOLVE_THREE + QUARTER
NUMBERS = TOP_THREE + QUARTER
FIELD = NUMBERS + 8
ZONE_ONE = FIELD + 2 * COLS
NEAR = ZONE_ONE + COLS
KEPT = (NEAR + 16, SKEL)
ORDER_ONE, ORDER_TWO, ORDER_THREE, PANEL_OF = range(0, 8, 2)

SOLVE_OWN, SOLVE_SIDE, SOLVE_ALL, TOP_ALL, COUPLE_ALL, SPREAD_ALL = 0, 1, 2, 3, 4, 6
COUPLE_FAR, SPREAD_FAR, ORDER_SIDE = 8, 11, 14
WHOLE = (ORDER_SIDE * SKEL + 8, SKEL)
SIDE_BLOCKS = 2 * COLS
SIDE_NUMBERS = SIDE_BLOCKS + 3 * SKEL
SIDE = (SIDE_NUMBERS + 8, SKEL)


def numbers_of(ref, row):
    return lanes(ref[row : row + 1], ref[row + 1 : row + 2]).astype(jnp.int32)


def block_of(ref, number):
    return ref[number * SKEL : (number + 1) * SKEL]


def start_kernel(*refs):
    count = len(NAMES)
    source = dict(zip(NAMES, refs[:count]))
    zone, base, row_out, side_out, kept = refs[count : count + 5]
    held = dict(zip(NAMES, refs[count + 5 : -1]))
    sems = refs[-1]
    here = Here()
    copies = {name: pltpu.make_async_copy(source[name], held[name], sems.at[i]) for i, name in enumerate(NAMES)}
    for name in NAMES:
        copies[name].start()

    def read(name):
        copies[name].wait()
        return held[name][...]

    rhs, leaf = read("rhs_nodes"), read("leaf_map")
    candidates = dot_t(rhs, leaf)
    kept[LEAF : LEAF + BOX] = leaf[:, :SKEL]
    kept[LEAF + BOX : LEAF + 2 * BOX] = leaf[:, SKEL:]
    picked = pick(candidates, read("order_one"))
    redund = picked[:, SKEL:]
    values = dot(redund, read("solve_one"))
    zone[...] = values
    kept[ZONE_ONE:NEAR] = values
    base[...] = picked[:, :SKEL] - dot(redund, read("interp_one"))
    spots = lax.broadcasted_iota(jnp.int32, (16, 9), 0) == lax.broadcasted_iota(jnp.int32, (16, 9), 1)
    near = jnp.where(spots, read("near_one").astype(jnp.float32), 0.0)
    kept[NEAR:] = jnp.broadcast_to(jnp.sum(near, axis=1, keepdims=True), VALUES)
    for name in NAMES[NAMES.index("couple_two") :]:
        copies[name].wait()
    for out, start in ((row_out.at[0], 0), (side_out, 0)):
        out[start : start + HALF] = held["solve_two"][...]
        out[start + HALF : start + HALF + QUARTER] = held["solve_three"][...]
        out[start + HALF + QUARTER : start + SKEL] = held["top_three"][...]
    cross = Here(crossed=True)

    def third(out, start, corner, edge_same, edge_else):
        corner = cross.block[corner[0]][corner[1]]
        edge = jnp.where(
            cross.same, cross.block[edge_same[0]][edge_same[1]], cross.block[edge_else[0]][edge_else[1]]
        )
        for i, (name, n) in enumerate(
            (("couple_three", corner), ("couple_three", edge), ("spread_three", corner), ("spread_three", edge))
        ):
            out[start + i * QUARTER : start + (i + 1) * QUARTER] = held[name][n]

    third(row_out.at[1], 0, (0, 0), (0, 1), (1, 0))
    third(side_out, SKEL, (0, 2), (1, 2), (0, 1))
    third(side_out, 2 * SKEL, (2, 0), (1, 0), (2, 1))
    for a in range(3):
        n = here.block[a][0]
        row_out[2 + a, :HALF] = held["couple_two"][n]
        row_out[2 + a, HALF:] = held["spread_two"][n]
    for a in range(3):
        for b in (1, 2):
            n = here.block[a][b]
            at = COUPLE_TWO + (2 * a + b - 1) * HALF
            kept[at : at + HALF] = held["couple_two"][n]
            at = SPREAD_TWO + (2 * a + b - 1) * HALF
            block = held["spread_two"][n]
            kept[at : at + HALF] = block + held["back_two"][...] if a == b == 1 else block
    edge = jnp.where(cross.same, cross.block[2][1], cross.block[1][2])
    for i, n in enumerate((4, cross.block[2][2], edge)):
        at = COUPLE_THREE + i * QUARTER
        kept[at : at + QUARTER] = held["couple_three"][n]
        at = SPREAD_THREE + i * QUARTER
        block = held["spread_three"][n]
        kept[at : at + QUARTER] = block + held["back_three"][...] if i == 0 else block
    for name, at in (
        ("interp_two", INTERP_TWO),
        ("solve_two", SOLVE_TWO),
        ("interp_three", INTERP_THREE),
        ("solve_three", SOLVE_THREE),
        ("top_three", TOP_THREE),
    ):
        kept[at : at + held[name].shape[0]] = held[name][...]
    for name, row in (
        ("order_one", ORDER_ONE),
        ("order_two", ORDER_TWO),
        ("order_three", ORDER_THREE),
        ("node_panel", PANEL_OF),
    ):
        numbers = held[name][...].astype(jnp.float32)
        kept[NUMBERS + row : NUMBERS + row + 1] = numbers[:, :SKEL]
        kept[NUMBERS + row + 1 : NUMBERS + row + 2] = numbers[:, SKEL:]
    side_out[3 * SKEL :] = kept[NUMBERS : NUMBERS + 8]
    kept[BACK_ONE : BACK_ONE + SKEL] = held["back_one"][...]
    field = dot(held["forward"][...], held["derivative"][...])
    kept[FIELD : FIELD + COLS] = field[:, :SKEL]
    kept[FIELD + COLS : FIELD + 2 * COLS] = field[:, SKEL:]


def side_kernel(pair, side, out):
    out[:COLS], out[COLS:SIDE_BLOCKS] = pair[0], pair[1]
    out[SIDE_BLOCKS:] = side[...]


def fill(here, boxes, chunk):
    for slot in range(4):
        chunk[slot, 0] = boxes[0]
        chunk[slot, 1] = jnp.where(here.slot_y == slot // 2, boxes[2], boxes[1])


def around(here, got, boxes, kept):
    out_x, out_y, out_xy = here.outside(got, (0,))
    out_x_row = jnp.where(here.edge_x, 0.0, got[here.along, 1])
    out_y_side = jnp.where(here.edge_y, 0.0, got[here.across, 1])
    grid = ((boxes[3], boxes[1], out_y_side), (boxes[2], boxes[0], out_y), (out_x_row, out_x, out_xy))
    grid = [[jnp.where(here.c == 1, grid[a][b], grid[2 - a][b]) for b in range(3)] for a in range(3)]
    grid = [[jnp.where(here.h == 1, row[b], row[2 - b]) for b in range(3)] for row in grid]
    return lanes(*[grid[k // 3][k % 3] * kept[NEAR + k : NEAR + k + 1] for k in range(9)])


def row_kernel(row, sides, chunk, boxes, out):
    here = Here()
    c, d = here.c, 1 - here.c
    for box, (member, number) in enumerate(((c, c), (d, d), (d, c), (c, d))):
        boxes[box] = sides[member, pl.ds(pl.multiple_of(number * COLS, COLS), COLS)]
    fill(here, boxes, chunk)
    out[0], out[1] = row[0], sides[d, SIDE_BLOCKS : SIDE_BLOCKS + SKEL]
    out[2], out[3] = row[1], sides[d, SIDE_BLOCKS + 2 * SKEL : SIDE_BLOCKS + 3 * SKEL]
    for a in range(3):
        out[4 + a] = row[2 + a]


def first_kernel(got, boxes, base, kept, couple, part):
    part[...] = base[...] - dot(around(Here(), got, boxes, kept), couple[...])


def put_together(here, kept, sides, row, whole):
    d = 1 - here.c
    mine, theirs = here.h * HALF, (1 - here.h) * HALF

    def put(number, offset, size, value):
        whole[pl.ds(pl.multiple_of(number * SKEL + offset, size), size)] = value

    def side(block, start, size):
        at = SIDE_BLOCKS + block * SKEL + start
        return sides[d, at : at + size]

    put(SOLVE_OWN, mine, HALF, kept[SOLVE_TWO : SOLVE_TWO + HALF])
    put(SOLVE_OWN, theirs, HALF, row[0, :HALF])
    put(SOLVE_SIDE, mine, HALF, side(0, 0, HALF))
    put(SOLVE_SIDE, theirs, HALF, row[1, :HALF])
    for a in range(3):
        for number, at, start in ((COUPLE_FAR, COUPLE_TWO, 0), (SPREAD_FAR, SPREAD_TWO, HALF)):
            at = at + (2 * a + 1) * HALF
            put(number + a, mine, HALF, kept[at : at + HALF])
            put(number + a, theirs, HALF, row[4 + a, start : start + HALF])
    own_at = (
        SOLVE_THREE,
        TOP_THREE,
        COUPLE_THREE + QUARTER,
        COUPLE_THREE + 2 * QUARTER,
        SPREAD_THREE + QUARTER,
        SPREAD_THREE + 2 * QUARTER,
    )
    for i in range(6):
        start = HALF + i * QUARTER if i < 2 else (i - 2) * QUARTER
        inverse = i < 2
        for c, h, value in (
            (here.c, here.h, kept[own_at[i] : own_at[i] + QUARTER]),
            (d, here.h, side(0 if inverse else 1, start, QUARTER)),
            (here.c, 1 - here.h, row[0 if inverse else 2, start : start + QUARTER]),
            (d, 1 - here.h, row[1 if inverse else 3, start : start + QUARTER]),
        ):
            put(SOLVE_ALL + i, (2 * c + h) * QUARTER, QUARTER, value)
    whole[ORDER_SIDE * SKEL :] = sides[d, SIDE_NUMBERS:]


def second_kernel(sums, kept, sides, row, chunk, base, zone, whole):
    here = Here()
    put_together(here, kept, sides, row, whole)
    c, d = here.c, 1 - here.c

    picked = pick(here.by_row(sums[c, c], sums[d, c]), numbers_of(kept, NUMBERS + ORDER_TWO))
    redund = picked[:, SKEL:]
    values = dot_t(redund, block_of(whole, SOLVE_OWN))
    zone[...] = values
    other = pick(here.by_row(sums[d, d], sums[c, d]), numbers_of(whole, ORDER_SIDE * SKEL + ORDER_TWO))
    other = dot_t(other[:, SKEL:], block_of(whole, SOLVE_SIDE))
    for slot in range(4):
        chunk[slot, 0] = values
        chunk[slot, 1] = other
    interp = kept[INTERP_TWO : INTERP_TWO + HALF]
    gone = dot_t(redund, stacked(interp, interp))
    base[...] = jnp.where(here.own_half(), picked[:, :SKEL] - gone, 0.0)


def second_part_kernel(near_at, far_at, got, chunk, base, kept, whole, part):
    here = Here()
    out_x, out_y, out_xy = here.outside(got, (0,))
    out_side = jnp.where(here.edge_y, 0.0, got[here.across, 1])
    near = jnp.zeros(VALUES, jnp.float32)
    far = jnp.zeros(VALUES, jnp.float32)
    for a, value, beyond in ((0, chunk[0, 1], out_side), (1, chunk[0, 0], out_y), (2, out_x, out_xy)):
        own = kept[near_at + 2 * a * HALF : near_at + (2 * a + 1) * HALF]
        near = near + dot_t(value, stacked(own, own))
        far = far + dot_t(beyond, block_of(whole, far_at + a))
    part[...] = base[...] - jnp.where(here.own_half(), near, 0.0) - far


def third_kernel(sums, kept, whole, chunk, base, zone):
    here = Here()
    joined = lanes(sums[0, 0] + sums[1, 0], sums[0, 1] + sums[1, 1])
    picked = pick(joined, numbers_of(kept, NUMBERS + ORDER_THREE))
    redund = picked[:, SKEL:]
    values = dot_t(redund, block_of(whole, SOLVE_ALL))
    zone[...] = values
    for slot in range(4):
        chunk[slot] = values
    gone = dot_t(redund, four(kept[INTERP_THREE : INTERP_THREE + QUARTER]))
    gone = gone + dot_t(values, four(kept[COUPLE_THREE : COUPLE_THREE + QUARTER]))
    base[...] = jnp.where(here.own_quarter(), picked[:, :SKEL] - gone, 0.0)


def third_part_kernel(at, got, base, whole, part):
    here = Here(crossed=True)
    out_x, out_y, out_xy = here.outside(got)
    edge = jnp.where(here.same, out_x, out_y)
    part[...] = base[...] - (dot_t(out_xy, block_of(whole, at)) + dot_t(edge, block_of(whole, at + 1)))


def total(sums):
    return (sums[0, 0] + sums[0, 1]) + (sums[1, 0] + sums[1, 1])


def top_kernel(sums, kept, whole, zone, chunk, base):
    here = Here()
    values = dot_t(total(sums), block_of(whole, TOP_ALL))
    for slot in range(4):
        chunk[slot] = values
    gone = dot_t(values, four(kept[SPREAD_THREE : SPREAD_THREE + QUARTER]))
    base[...] = jnp.where(here.own_quarter(), zone[...] - gone, 0.0)


def back_three_kernel(sums, values, kept, zone, chunk, base):
    here = Here()
    final = place(lanes(values[0], total(sums)), numbers_of(kept, NUMBERS + ORDER_THREE))
    low, high = final[:, :SKEL], final[:, SKEL:]
    own = jnp.where(here.c == 0, low, high)
    other = jnp.where(here.c == 0, high, low)
    for slot in range(4):
        chunk[slot, 0] = own
        chunk[slot, 1] = other
    base[...] = jnp.where(here.own_half(), zone[...], 0.0)


def back_two_kernel(sums, values, kept, whole, chunk, boxes):
    here = Here()
    c, d = here.c, 1 - here.c
    own = lanes(values[0, 0], sums[0, c] + sums[1, c])
    own = place(own, numbers_of(kept, NUMBERS + ORDER_TWO))
    other = lanes(values[0, 1], sums[0, d] + sums[1, d])
    other = place(other, numbers_of(whole, ORDER_SIDE * SKEL + ORDER_TWO))

    def rows_of(final):
        low, high = final[:, :SKEL], final[:, SKEL:]
        return jnp.where(here.h == 0, low, high), jnp.where(here.h == 0, high, low)

    value, value_row = rows_of(own)
    value_side, value_diag = rows_of(other)
    boxes[0], boxes[1], boxes[2], boxes[3] = value, value_side, value_row, value_diag
    fill(here, boxes, chunk)


def last_kernel(got, boxes, kept, spread, adjoint, shares):
    here = Here()
    rest = kept[ZONE_ONE:NEAR] - dot(around(here, got, boxes, kept), spread[...])
    rest = rest - dot(boxes[0], kept[BACK_ONE : BACK_ONE + SKEL])
    final = place(lanes(boxes[0], rest), numbers_of(kept, NUMBERS + ORDER_ONE))
    result = lanes(dot(final, kept[LEAF : LEAF + BOX]), dot(final, kept[LEAF + BOX : LEAF + 2 * BOX]))
    adjoint[...] = result
    field = lanes(kept[FIELD : FIELD + COLS], kept[FIELD + COLS : FIELD + 2 * COLS])
    count = lax.axis_size("rhs")
    weight = jnp.sum(result * field, axis=0, keepdims=True) / (count * COLS)
    share = PANELS // count
    number = lax.broadcasted_iota(jnp.int32, (SKEL, BOX), 0)
    panels = numbers_of(kept, NUMBERS + PANEL_OF)
    weight = jnp.broadcast_to(weight, (COLS, BOX))
    for r in range(count):
        inside = (number < share) & (panels == number + r * share)
        inside = jnp.where(inside, 1.0, 0.0).astype(jnp.bfloat16)
        shares[r] = dims(weight, (inside,), 1)[:8]


def end_kernel(adjoint, shares, adjoint_out, gradient_out):
    adjoint_out[...] = adjoint[...]
    total = shares[0, 0:1] + shares[1, 0:1]
    for r in range(2, shares.shape[0]):
        total = total + shares[r, 0:1]
    gradient_out[...] = total[:, : gradient_out.shape[1]]


def spec(space, count):
    return [pl.BlockSpec(memory_space=space)] * count


def call(body, outs, *operands):
    outs = tuple(pltpu.VMEM(shape, jnp.float32) for shape in outs)
    result = pl.pallas_call(
        body,
        out_shape=outs,
        in_specs=spec(pltpu.VMEM, len(operands)),
        out_specs=tuple(spec(pltpu.VMEM, len(outs))),
        compiler_params=pltpu.CompilerParams(vmem_limit_bytes=VMEM_LIMIT),
    )(*[pltpu.with_memory_space_constraint(operand, pltpu.VMEM) for operand in operands])
    return result if len(outs) > 1 else result[0]


def start(arrays):
    outs = [
        pltpu.VMEM(shape, jnp.float32)
        for shape in (VALUES, VALUES, (5, *BLOCK), (3 * SKEL + 8, SKEL), KEPT)
    ]
    return pl.pallas_call(
        start_kernel,
        out_shape=tuple(outs),
        in_specs=spec(pl.ANY, len(NAMES)),
        out_specs=tuple(spec(pltpu.VMEM, len(outs))),
        scratch_shapes=[pltpu.VMEM(arrays[name].shape, arrays[name].dtype) for name in NAMES]
        + [pltpu.SemaphoreType.DMA((len(NAMES),))],
        compiler_params=pltpu.CompilerParams(vmem_limit_bytes=VMEM_LIMIT),
    )(*[pltpu.with_memory_space_constraint(arrays[name], pltpu.HBM) for name in NAMES])


def on_device(groups, *arguments):
    arrays = {}
    for name, value in zip(GIVEN, arguments):
        value = value[0] if value.ndim == 3 else value[0, 0]
        if value.shape[-1] in (HALF, QUARTER):
            value = jnp.swapaxes(value, -1, -2)
        arrays[name] = value

    def outside(chunk, crossed=False):
        members = groups.crossed if crossed else groups.shifted
        return lax.all_to_all(chunk, AXES, 0, 0, axis_index_groups=members)

    def shared(part):
        pair = lax.all_gather(part, AXES, axis_index_groups=groups.diagonal)
        return lax.all_gather(pair, AXES, axis_index_groups=groups.sibling)

    def from_row(blocks):
        return lax.ppermute(blocks, "by", [(i, i ^ 1) for i in range(lax.axis_size("by"))])

    couple, spread = (arrays[name].reshape(9 * SKEL, SKEL) for name in ("couple_one", "spread_one"))
    zone_one, base, to_row, to_side, kept = start(arrays)
    pair = lax.all_gather(zone_one, AXES, axis_index_groups=groups.diagonal)
    to_side = call(side_kernel, [SIDE], pair, to_side)
    sides = lax.all_gather(to_side, AXES, axis_index_groups=groups.sibling)
    chunk, boxes, to_row = call(
        row_kernel, [(4, 2, *VALUES), (4, *VALUES), (7, *BLOCK)], to_row, sides
    )
    row = from_row(to_row)
    part = call(first_kernel, [VALUES], outside(chunk), boxes, base, kept, couple)

    one, two, three = [(4, *VALUES), VALUES, VALUES], [(4, 2, *VALUES), VALUES, VALUES], [VALUES]
    chunk, base, zone_two, whole = call(second_kernel, two + [WHOLE], shared(part), kept, sides, row)
    down_two = functools.partial(second_part_kernel, COUPLE_TWO, COUPLE_FAR)
    part = call(down_two, three, outside(chunk), chunk, base, kept, whole)
    chunk, base, zone_three = call(third_kernel, one, shared(part), kept, whole)
    down_three = functools.partial(third_part_kernel, COUPLE_ALL)
    part = call(down_three, three, outside(chunk, True), base, whole)
    chunk, base = call(top_kernel, one[:2], shared(part), kept, whole, zone_three)
    up_three = functools.partial(third_part_kernel, SPREAD_ALL)
    part = call(up_three, three, outside(chunk, True), base, whole)
    chunk, base = call(back_three_kernel, two[:2], shared(part), chunk, kept, zone_two)
    up_two = functools.partial(second_part_kernel, SPREAD_TWO, SPREAD_FAR)
    part = call(up_two, three, outside(chunk), chunk, base, kept, whole)
    chunk, boxes = call(back_two_kernel, [(4, 2, *VALUES), (4, *VALUES)], shared(part), chunk, kept, whole)
    count = lax.axis_size("rhs")
    adjoint, shares = call(last_kernel, [(COLS, BOX), (count, 8, SKEL)], outside(chunk), boxes, kept, spread)
    shares = lax.all_to_all(shares, "rhs", 0, 0)
    adjoint, gradient = pl.pallas_call(
        end_kernel,
        out_shape=(
            jax.ShapeDtypeStruct((COLS, BOX), jnp.float32),
            jax.ShapeDtypeStruct((1, PANELS // count), jnp.float32),
        ),
        in_specs=spec(pltpu.VMEM, 2),
        out_specs=tuple(spec(pltpu.VMEM, 2)),
        compiler_params=pltpu.CompilerParams(vmem_limit_bytes=VMEM_LIMIT),
    )(*[pltpu.with_memory_space_constraint(operand, pltpu.VMEM) for operand in (adjoint, shares)])
    return adjoint[None, None], gradient[None]


def solution(mesh):
    box = P("bx", "by")
    columns = P("bx", "by", "rhs", None)
    groups = Groups(mesh.shape["bx"], mesh.shape["by"], mesh.shape["rhs"])
    return jax.shard_map(
        functools.partial(on_device, groups),
        mesh=mesh,
        in_specs=(columns, columns) + (box,) * 23,
        out_specs=(columns, P("bx", "by", "rhs")),
        check_vma=False,
    )
```
